128 devices in a mesh: ctx: 8 (over x_hi, z), batch: 16 (over x_lo, y, core).
Axes of the slice: x: 4 (x_hi: 2, x_lo: 2; x = x_hi * 2 + x_lo), y: 4, z: 4, core: 2. Of those that a mesh axis runs over, the one named last changes fastest.
Arguments:
- queries: bfloat16 [768, 8192], P('batch', 'ctx'), may hold values from -24 to 24
- new_key: bfloat16 [768, 1024], P('batch', 'ctx'), may hold values from -16 to 16
- new_value: bfloat16 [768, 1024], P('batch', 'ctx'), may hold values from -6 to 6
- prefix_keys: bfloat16 [16384, 1024], P('ctx'), may hold values from -9 to 9
- prefix_values: bfloat16 [16384, 1024], P('ctx'), may hold values from -8 to 8
- suffix_keys: bfloat16 [768, 128, 1024], P('batch', None, 'ctx'), may hold values from -16 to 16
- suffix_values: bfloat16 [768, 128, 1024], P('batch', None, 'ctx'), may hold values from -6 to 6
- suffix_lengths: int32 [768], P('batch'), may hold values from 1 to 128, as said below
- out_weight: bfloat16 [8192, 8192], P('ctx', 'batch'), may hold values from -0.0625 to 0.0625
- residual: bfloat16 [768, 8192], P(None, 'batch'), may hold values from -8 to 8
- norm_gain: bfloat16 [8192], P('batch'), may hold values from 0.3984375 to 1.1953125
- gate_weight: bfloat16 [8192, 28672], P('batch', 'ctx'), may hold values from -0.0625 to 0.0625
- up_weight: bfloat16 [8192, 28672], P('batch', 'ctx'), may hold values from -0.0625 to 0.0625
Outputs:
- stream: bfloat16 [768, 8192], P(None, 'batch')
- activation: bfloat16 [768, 28672], P('batch', 'ctx')
The draws below stay inside these ranges and needn't reach their ends.
Inputs may be any that keep to these rules, and one draw needn't show every extreme that they name: `suffix_lengths`: each leaf has between 1 and 128 filled suffix slots, the first ones; some leaf has exactly 128 and some leaf exactly 1.
All inputs are finite; a program needn't handle non-finite values.
Results may differ from the reference program's by a relative error of at most 0.025.
Values may be sent and summed in bfloat16 or wider, within the bound.
No kernel may reach another device: no remote copies, remote signals or barrier semaphores. Data moves between devices by JAX's collectives and lax.ppermute only.
A program may use at most 128 MiB of HBM per device.

```python
import math
import jax
import jax.numpy as jnp
from jax import lax

D = 8192
HEADS = 64
KV = 8
HD = 128
FF = 28672
PREFIX = 16384
SUF = 128
GROUP = 8
LEAVES = 768


def shared_direction(key):
    flips = jax.random.bernoulli(jax.random.fold_in(key, 101), 0.5, (HD,))
    return jnp.where(flips, 1.0, -1.0).astype(jnp.float32)


def draw_queries(key, part):
    direction = shared_direction(key)
    key = jax.random.fold_in(key, 1)
    shape = (LEAVES, HEADS * HD)
    base = jnp.clip(jax.random.normal(key, shape, jnp.float32), -6.0, 6.0)
    target = 150.0 + 130.0 * jax.random.uniform(jax.random.fold_in(key, 2), (LEAVES, 1), jnp.float32)
    strength = target / (3.0 * jnp.sqrt(jnp.float32(HD)))
    chosen = jnp.arange(LEAVES, dtype=jnp.int32)[:, None] % 7 == 3
    aligned_rows = jnp.tile(direction, HEADS)[None, :] * strength
    base = jnp.where(chosen, aligned_rows, base)
    return base.astype(jnp.bfloat16)


def draw_prefix_keys(key, part):
    direction = shared_direction(key)
    key = jax.random.fold_in(key, 3)
    shape = (PREFIX, KV * HD)
    base = jnp.clip(1.6 * jax.random.normal(key, shape, jnp.float32), -8.0, 8.0)
    spot = jax.random.randint(jax.random.fold_in(key, 4), (), 0, PREFIX - 1)
    place = jnp.arange(PREFIX, dtype=jnp.int32)[:, None]
    row = jnp.tile(direction, KV)[None, :]
    base = jnp.where(place == spot, 6.0 * row, base)
    base = jnp.where(place == spot + 1, 5.96875 * row, base)
    return base.astype(jnp.bfloat16)


def draw_prefix_values(key, part):
    key = jax.random.fold_in(key, 5)
    means = jnp.clip(jax.random.normal(jax.random.fold_in(key, 6), (64, KV * HD), jnp.float32), -3.0, 3.0)
    region = jnp.arange(PREFIX, dtype=jnp.int32) // (PREFIX // 64)
    spread = means[region]
    noise = jnp.clip(3.5 * jax.random.normal(key, (PREFIX, KV * HD), jnp.float32), -8.0, 8.0)
    return jnp.clip(spread + noise, -8.0, 8.0).astype(jnp.bfloat16)


def draw_suffix_keys(key, part):
    direction = shared_direction(key)
    key = jax.random.fold_in(key, 14)
    shape = (LEAVES, SUF, KV * HD)
    base = jnp.clip(3.0 * jax.random.normal(key, shape, jnp.float32), -16.0, 16.0)
    chosen = jnp.arange(LEAVES, dtype=jnp.int32)[:, None, None] % 7 == 3
    first_slot = jnp.arange(SUF, dtype=jnp.int32)[None, :, None] == 0
    row = jnp.tile(direction, KV)[None, None, :] * 6.03125
    base = jnp.where(chosen & first_slot, row, base)
    return base.astype(jnp.bfloat16)


def draw_residual(key, part):
    key = jax.random.fold_in(key, 8)
    rows = jnp.exp(jax.random.uniform(jax.random.fold_in(key, 9), (LEAVES, 1), jnp.float32, jnp.log(0.2), jnp.log(2.0)))
    cols = jnp.exp(jax.random.uniform(jax.random.fold_in(key, 10), (1, D), jnp.float32, jnp.log(0.5), jnp.log(1.5)))
    cols = cols * (0.5 + jnp.arange(D, dtype=jnp.float32)[None, :] / D)
    noise = jnp.clip(jax.random.normal(key, (LEAVES, D), jnp.float32), -4.0, 4.0)
    return jnp.clip(noise * rows * cols, -8.0, 8.0).astype(jnp.bfloat16)


def draw_suffix_lengths(key, part):
    key = jax.random.fold_in(key, 7)
    lengths = jax.random.randint(key, (LEAVES,), 1, SUF + 1)
    first = jax.random.randint(jax.random.fold_in(key, 12), (), 0, LEAVES)
    step = jax.random.randint(jax.random.fold_in(key, 13), (), 0, LEAVES - 1)
    second = (first + 1 + step) % LEAVES
    lengths = lengths.at[first].set(SUF)
    lengths = lengths.at[second].set(1)
    return lengths.astype(jnp.int32)


def block_scale(key, dims, shards, smallest, top_value):
    level = 1.0
    for dim, blocks in shards:
        draws = jax.random.uniform(jax.random.fold_in(jax.random.fold_in(key, 6), dim), (blocks,), jnp.float32, smallest / len(shards), top_value / len(shards))
        level = level * jnp.repeat(jnp.exp(draws), dims[dim] // blocks).reshape((-1,) + (1,) * (len(dims) - 1 - dim))
    return level


def bell_draw(rng, extent, scale, reach, cuts=(), held_as=jnp.bfloat16):
    result = jax.random.normal(rng, extent, jnp.float32) * scale
    if len(cuts) > 0:
        result = block_scale(rng, extent, cuts, -0.22, 0.18) * result
    return jnp.clip(result, min=-reach, max=reach).astype(held_as)


def setup_inputs(seed: int = 0) -> dict:
    splits = jax.random.split(jax.random.key(seed), 14)
    return {
        "queries": draw_queries(jax.random.fold_in(splits[13], 71), 0),
        "new_key": bell_draw(splits[1], (LEAVES, KV * HD), 4.0, 16.0, ((0, 16), (1, 8))),
        "new_value": bell_draw(splits[2], (LEAVES, KV * HD), 1.0, 6.0, ((0, 16), (1, 8))),
        "prefix_keys": draw_prefix_keys(jax.random.fold_in(splits[13], 71), 0),
        "prefix_values": draw_prefix_values(jax.random.fold_in(splits[13], 71), 0),
        "suffix_keys": draw_suffix_keys(jax.random.fold_in(splits[13], 71), 0),
        "suffix_values": bell_draw(splits[6], (LEAVES, SUF, KV * HD), 1.0, 6.0, ((0, 16), (2, 8))),
        "suffix_lengths": draw_suffix_lengths(jax.random.fold_in(splits[13], 71), 0),
        "out_weight": bell_draw(splits[8], (HEADS * HD, D), (HEADS * HD) ** -0.5, 0.0625, ((0, 8), (1, 16))),
        "residual": draw_residual(jax.random.fold_in(splits[13], 71), 0),
        "norm_gain": jnp.clip(jnp.exp(math.log(1.1953125) - 1.0986123 * jax.random.uniform(splits[10], (D,), jnp.float32) ** block_scale(splits[10], (D,), ((0, 16),), -0.2, 0.2)), 0.3984375, 1.1953125).astype(jnp.bfloat16),
        "gate_weight": bell_draw(splits[11], (D, FF), D ** -0.5, 0.0625, ((0, 16), (1, 8))),
        "up_weight": bell_draw(splits[12], (D, FF), D ** -0.5, 0.0625, ((0, 16), (1, 8))),
    }


def attend_block(block):
    query_rows, fresh_key, value_new, key_suf, value_suf, lengths, key_pre, value_pre = block
    count = query_rows.shape[0]
    score_scale = 1.0 / jnp.sqrt(jnp.float32(HD))
    query_vector = query_rows.astype(jnp.float32).reshape(count, KV, GROUP, HD)
    pre_scores = jnp.einsum('bkgd,pkd->bkgp', query_vector, key_pre) * score_scale
    suf_scores = jnp.einsum('bkgd,bskd->bkgs', query_vector, key_suf.astype(jnp.float32)) * score_scale
    valid = jnp.arange(SUF, dtype=jnp.int32)[None, :] < lengths[:, None]
    suf_scores = jnp.where(valid[:, None, None, :], suf_scores, jnp.float32(-1e+30))
    fresh_scores = jnp.einsum('wpvz,wpz->wpv', query_vector, fresh_key.astype(jnp.float32)) * score_scale
    top = jnp.maximum(jnp.maximum(lax.optimization_barrier(jnp.max(pre_scores, -1)), lax.optimization_barrier(jnp.max(suf_scores, -1))), fresh_scores)
    pre_w = jnp.exp(pre_scores - top[..., None])
    suf_w = jnp.exp(suf_scores - top[..., None])
    new_w = jnp.exp(fresh_scores - top)
    total = lax.optimization_barrier(jnp.sum(pre_w, -1)) + lax.optimization_barrier(jnp.sum(suf_w, -1)) + new_w
    pre_r = pre_w.astype(jnp.bfloat16).astype(jnp.float32)
    suf_r = suf_w.astype(jnp.bfloat16).astype(jnp.float32)
    new_r = new_w.astype(jnp.bfloat16).astype(jnp.float32)
    numer = jnp.einsum('bkgp,pkd->bkgd', pre_r, value_pre)
    numer = numer + jnp.einsum('bkgs,bskd->bkgd', suf_r, value_suf.astype(jnp.float32))
    numer = numer + new_r[..., None] * value_new.astype(jnp.float32)[:, :, None, :]
    attended = (numer / total[..., None]).astype(jnp.bfloat16)
    return attended.reshape(count, HEADS * HD)

def reference(queries, new_key, new_value, prefix_keys, prefix_values, suffix_keys, suffix_values, suffix_lengths, out_weight, residual, norm_gain, gate_weight, up_weight):
    blocks = LEAVES // 8
    key_pre = prefix_keys.astype(jnp.float32).reshape(PREFIX, KV, HD)
    value_pre = prefix_values.astype(jnp.float32).reshape(PREFIX, KV, HD)

    def one_block(index):
        start = index * 8
        pieces = (lax.dynamic_slice_in_dim(queries, start, 8, 0), lax.dynamic_slice_in_dim(new_key, start, 8, 0).reshape(8, KV, HD), lax.dynamic_slice_in_dim(new_value, start, 8, 0).reshape(8, KV, HD), lax.dynamic_slice_in_dim(suffix_keys, start, 8, 0).reshape(8, SUF, KV, HD), lax.dynamic_slice_in_dim(suffix_values, start, 8, 0).reshape(8, SUF, KV, HD), lax.dynamic_slice_in_dim(suffix_lengths, start, 8, 0), key_pre, value_pre)
        return attend_block(pieces)
    attended = lax.map(one_block, jnp.arange(blocks, dtype=jnp.int32)).reshape(LEAVES, HEADS * HD)
    mixed = jnp.dot(attended, out_weight, preferred_element_type=jnp.float32)
    stream = (residual.astype(jnp.float32) + mixed).astype(jnp.bfloat16)
    wide = stream.astype(jnp.float32)
    rms = jnp.sqrt(lax.optimization_barrier(jnp.mean(wide * wide, axis=1)) + 1e-05)
    scaled = (wide * norm_gain.astype(jnp.float32)[None, :]).astype(jnp.bfloat16)
    gate = jnp.dot(scaled, gate_weight, preferred_element_type=jnp.float32) / rms[:, None]
    up = jnp.dot(scaled, up_weight, preferred_element_type=jnp.float32) / rms[:, None]
    activation = (jax.nn.silu(gate) * up).astype(jnp.bfloat16)
    return (stream, activation)
```

```python
import jax
import jax.numpy as jnp
from jax import lax
from jax.experimental import pallas as pl
from jax.experimental.pallas import tpu as pltpu
from jax.sharding import PartitionSpec as P

D = 8192
KV = 8
HD = 128
SUF = 128
GROUP = 8
ROWS = 48
QROWS = ROWS * GROUP
META = 16
PAYLOAD = QROWS + QROWS // 128 * META
PRE = 2048
HALF = 512
HIDDEN = 3584
A_COLS = 1536
B_COLS = HIDDEN - A_COLS
TILE = 512
BF = jnp.bfloat16
F32 = jnp.float32
VMEM = 48 * 1024 * 1024


def ctx_perm(flip, s):
    return [(x * 4 + z, (x ^ flip) * 4 + (z + s) % 4) for x in range(2) for z in range(4)]


def batch_perm(flip_x, s, flip_core):
    return [
        (x * 8 + y * 2 + k, (x ^ flip_x) * 8 + (y + s) % 4 * 2 + (k ^ flip_core))
        for x in range(2)
        for y in range(4)
        for k in range(2)
    ]


def over_ctx(v, flip, s):
    return lax.ppermute(v, "ctx", ctx_perm(flip, s))


def over_batch(v, flip_x, s, flip_core=0):
    return lax.ppermute(v, "batch", batch_perm(flip_x, s, flip_core))


def nt_dot(a, b):
    return lax.dot_general(a, b, (((1,), (1,)), ((), ())), preferred_element_type=F32)


def heads_as_rows(q):
    return jnp.concatenate([q[:, h * HD : (h + 1) * HD] for h in range(GROUP)], axis=0)


def split3(v):
    hi = v.astype(BF).astype(F32)
    rest = v - hi
    mid = rest.astype(BF).astype(F32)
    return hi, mid, rest - mid


def prefix_kernel(group_ref, q_ref, k_ref, v_ref, first_ref, second_ref):
    scale = 1.0 / (HD**0.5)
    q = heads_as_rows(q_ref[0])
    k = k_ref[...]
    v = v_ref[...]
    outs, metas = [], []
    column = lax.broadcasted_iota(jnp.int32, (128, 128), 1)
    for t in range(QROWS // 128):
        s = nt_dot(q[t * 128 : (t + 1) * 128], k)
        top = jnp.max(s, axis=1, keepdims=True)
        w = jnp.exp((s - top) * scale)
        total = jnp.sum(w, axis=1, keepdims=True)
        o = jnp.dot(w.astype(BF), v, preferred_element_type=F32)
        outs.append((o / total).astype(BF))
        hi, mid, lo = split3(top * scale + jnp.log(total))
        parts = jnp.where(column == 0, hi, jnp.where(column == 1, mid, jnp.where(column == 2, lo, 0.0)))
        metas.append(parts.T[:META].astype(BF))

    def put(ref):
        for t in range(QROWS // 128):
            ref[t * 128 : (t + 1) * 128, :] = outs[t]
            ref[QROWS + t * META : QROWS + (t + 1) * META, :] = metas[t]

    @pl.when(pl.program_id(0) == 0)
    def _():
        put(first_ref)

    @pl.when(pl.program_id(0) == 1)
    def _():
        put(second_ref)


def prefix_pair(groups, q2, keys, values):
    shape = jax.ShapeDtypeStruct((PAYLOAD, HD), BF)
    return pl.pallas_call(
        prefix_kernel,
        grid_spec=pltpu.PrefetchScalarGridSpec(
            num_scalar_prefetch=1,
            grid=(2,),
            in_specs=[
                pl.BlockSpec((1, ROWS, GROUP * HD), lambda i, g: (i, 0, 0)),
                pl.BlockSpec((PRE, HD), lambda i, g: (0, g[i])),
                pl.BlockSpec((PRE, HD), lambda i, g: (0, g[i])),
            ],
            out_specs=[pl.BlockSpec((PAYLOAD, HD), lambda i, g: (0, 0))] * 2,
        ),
        out_shape=[shape, shape],
        compiler_params=pltpu.CompilerParams(vmem_limit_bytes=VMEM),
        cost_estimate=pl.CostEstimate(
            flops=2 * 4 * QROWS * PRE * HD, bytes_accessed=2 * 2 * 2 * PRE * HD, transcendentals=2 * QROWS * PRE
        ),
        name="prefix_pair",
    )(groups, q2, keys, values)


SUF_LEAVES = 16


def suffix_kernel(q_ref, k_ref, v_ref, nk_ref, nv_ref, len_ref, o_ref, lse_ref):
    scale = 1.0 / (HD**0.5)
    n = SUF_LEAVES * GROUP
    q = heads_as_rows(q_ref[...])
    s = nt_dot(q, k_ref[...]) * scale
    lengths = jnp.concatenate([len_ref[...][:, :1]] * GROUP, axis=0)
    row = lax.broadcasted_iota(jnp.int32, (n, 1), 0) % SUF_LEAVES
    slot = lax.broadcasted_iota(jnp.int32, s.shape, 1) - row * SUF
    s = jnp.where((slot >= 0) & (slot < lengths), s, -1e30)
    fresh_key = jnp.concatenate([nk_ref[...].astype(F32)] * GROUP, axis=0)
    fresh = jnp.sum(q.astype(F32) * fresh_key, axis=1, keepdims=True) * scale
    top = jnp.maximum(jnp.max(s, axis=1, keepdims=True), fresh)
    w = jnp.exp(s - top)
    wn = jnp.exp(fresh - top)
    total = jnp.sum(w, axis=1, keepdims=True) + wn
    o = jnp.dot(w.astype(BF), v_ref[...], preferred_element_type=F32)
    fresh_value = jnp.concatenate([nv_ref[...].astype(F32)] * GROUP, axis=0)
    o = (o + wn.astype(BF).astype(F32) * fresh_value) / total
    lse = jnp.broadcast_to(top + jnp.log(total), o.shape)
    for h in range(GROUP):
        o_ref[h] = o[h * SUF_LEAVES : (h + 1) * SUF_LEAVES]
        lse_ref[h] = lse[h * SUF_LEAVES : (h + 1) * SUF_LEAVES]


def suffix_part(q, keys, values, new_key, new_value, lengths):
    shape = jax.ShapeDtypeStruct((GROUP, ROWS, HD), F32)
    leaf = lambda w: pl.BlockSpec((SUF_LEAVES, w), lambda i: (i, 0))
    cached = pl.BlockSpec((SUF_LEAVES * SUF, HD), lambda i: (i, 0))
    return pl.pallas_call(
        suffix_kernel,
        grid=(ROWS // SUF_LEAVES,),
        in_specs=[leaf(GROUP * HD), cached, cached, leaf(HD), leaf(HD), leaf(HD)],
        out_specs=[pl.BlockSpec((GROUP, SUF_LEAVES, HD), lambda i: (0, i, 0))] * 2,
        out_shape=[shape, shape],
        compiler_params=pltpu.CompilerParams(vmem_limit_bytes=VMEM),
        cost_estimate=pl.CostEstimate(flops=4 * QROWS * 2048 * HD, bytes_accessed=4 << 20, transcendentals=QROWS * 2048),
        name="suffix_part",
    )(
        q,
        keys.reshape(ROWS * SUF, HD),
        values.reshape(ROWS * SUF, HD),
        new_key,
        new_value,
        jnp.broadcast_to(lengths[:, None], (ROWS, HD)),
    )


def merge_kernel(*refs):
    parts, (so_ref, sl_ref, out_ref, held) = refs[:8], refs[8:]
    for t in range(QROWS // 128):
        rows = []
        for p in parts:
            m = p[QROWS + t * META : QROWS + (t + 1) * META, :].astype(F32)
            rows.append(m[0:1] + m[1:2] + m[2:3])
        lse = jnp.concatenate(rows, axis=0).T
        suf_lse = sl_ref[t * 128 : (t + 1) * 128, :1]
        top = jnp.maximum(jnp.max(lse, axis=1, keepdims=True), suf_lse)
        w = jnp.exp(lse - top)
        ws = jnp.exp(suf_lse - top)
        total = jnp.sum(w, axis=1, keepdims=True) + ws
        o = so_ref[t * 128 : (t + 1) * 128, :] * ws
        for i, p in enumerate(parts):
            o = o + p[t * 128 : (t + 1) * 128, :].astype(F32) * w[:, i : i + 1]
        held[t * 128 : (t + 1) * 128, :] = (o / total).astype(BF)
    for h in range(GROUP):
        out_ref[:, h * HD : (h + 1) * HD] = held[h * ROWS : (h + 1) * ROWS, :]


def merge_parts(parts, suffix_out, suffix_lse):
    return pl.pallas_call(
        merge_kernel,
        out_shape=jax.ShapeDtypeStruct((ROWS, GROUP * HD), BF),
        scratch_shapes=[pltpu.VMEM((QROWS, HD), BF)],
        compiler_params=pltpu.CompilerParams(vmem_limit_bytes=VMEM),
        cost_estimate=pl.CostEstimate(flops=QROWS * HD * 20, bytes_accessed=2 << 20, transcendentals=QROWS * 10),
        name="merge_parts",
    )(*parts, suffix_out.reshape(QROWS, HD), suffix_lse.reshape(QROWS, HD))


def project_kernel(z_ref, a_ref, own_w_ref, other_w_ref, mine_ref, *send_refs):
    z = z_ref[0]
    pieces = [a_ref[pl.ds(pl.multiple_of((z + s) % 4 * 96, 16), 96), :] for s in range(4)]
    a = jnp.concatenate(pieces, axis=0)
    for half, w_ref in enumerate((own_w_ref, other_w_ref)):
        y = jnp.dot(a, w_ref[...], preferred_element_type=F32)
        at = slice(half * HALF, (half + 1) * HALF)
        mine_ref[:, at] = y[:96]
        for s, ref in enumerate(send_refs):
            ref[:, at] = y[(s + 1) * 96 : (s + 2) * 96].astype(BF)


def project(z, attended, own_w, other_w):
    vmem = pl.BlockSpec(memory_space=pltpu.VMEM)
    return pl.pallas_call(
        project_kernel,
        in_specs=[pl.BlockSpec(memory_space=pltpu.SMEM), vmem, vmem, vmem],
        out_specs=[vmem] * 4,
        out_shape=[jax.ShapeDtypeStruct((96, 2 * HALF), F32)] + [jax.ShapeDtypeStruct((96, 2 * HALF), BF)] * 3,
        compiler_params=pltpu.CompilerParams(vmem_limit_bytes=VMEM),
        cost_estimate=pl.CostEstimate(flops=2 * 384 * 1024 * 1024, bytes_accessed=4 << 20, transcendentals=0),
        name="project",
    )(z, attended, own_w, other_w)


def fill_kernel(place_ref, *refs):
    pieces, (gain_ref, scaled_ref, squares_ref) = refs[:4], refs[4:]
    for j, piece in enumerate(pieces):
        for e in range(2):
            at = pl.multiple_of(place_ref[j * 2 + e] * ROWS, 16)
            wide = piece[e * ROWS : (e + 1) * ROWS, :].astype(F32)
            scaled_ref[pl.ds(at, ROWS), :] = (wide * gain_ref[...]).astype(BF)
            squares_ref[pl.ds(at, ROWS), :] = jnp.broadcast_to(jnp.sum(wide * wide, axis=1, keepdims=True), (ROWS, HD))


def fill(place, pieces, gain):
    vmem = pl.BlockSpec(memory_space=pltpu.VMEM)
    return pl.pallas_call(
        fill_kernel,
        in_specs=[pl.BlockSpec(memory_space=pltpu.SMEM)] + [vmem] * 5,
        out_specs=[vmem] * 2,
        out_shape=[jax.ShapeDtypeStruct((384, 2 * HALF), BF), jax.ShapeDtypeStruct((384, HD), F32)],
        compiler_params=pltpu.CompilerParams(vmem_limit_bytes=VMEM),
        cost_estimate=pl.CostEstimate(flops=384 * 4096, bytes_accessed=2 << 20, transcendentals=0),
        name="scale_rows",
    )(place, *pieces, gain)


def hidden_sums(s_ref, weights):
    s = s_ref[...]
    out = []
    for own, other in (weights[:2], weights[2:]):
        y = jnp.dot(s[:, :HALF], own[...], preferred_element_type=F32)
        out.append(y + jnp.dot(s[:, HALF:], other[...], preferred_element_type=F32))
    return out


def x_first_kernel(s_ref, g0, g1, u0, u1, keep_ref, send_ref):
    for n, y in enumerate(hidden_sums(s_ref, (g0, g1, u0, u1))):
        for k in range(4):
            keep_ref[k, n] = y[k * ROWS : (k + 1) * ROWS]
            send_ref[k, n] = y[(4 + k) * ROWS : (5 + k) * ROWS].astype(BF)


def y_first_kernel(s_ref, g0, g1, u0, u1, here_ref, up_ref, down_ref, far_gate_ref, far_up_ref):
    for n, y in enumerate(hidden_sums(s_ref, (g0, g1, u0, u1))):
        for x in range(2):
            at = slice(x * ROWS, (x + 1) * ROWS)
            part = [y[(x * 4 + k) * ROWS : (x * 4 + k + 1) * ROWS] for k in range(4)]
            here_ref[n, at, :] = part[0]
            up_ref[n, at, :] = part[1]
            down_ref[n, at, :] = part[3]
            (far_gate_ref, far_up_ref)[n][at, :] = part[2].astype(BF)


def hidden_call(kernel, first_tile, tiles, scaled, weights, out_specs, out_shape, name):
    weight = pl.BlockSpec((HALF, TILE), lambda j: (0, j + first_tile))
    return pl.pallas_call(
        kernel,
        grid=(tiles,),
        in_specs=[pl.BlockSpec((384, 2 * HALF), lambda j: (0, 0))] + [weight] * 4,
        out_specs=out_specs,
        out_shape=out_shape,
        compiler_params=pltpu.CompilerParams(vmem_limit_bytes=VMEM),
        cost_estimate=pl.CostEstimate(
            flops=2 * 384 * 1024 * 1024 * tiles, bytes_accessed=(4 << 20) * tiles, transcendentals=0
        ),
        name=name,
    )(scaled, *weights)


def x_first(scaled, weights):
    spec = pl.BlockSpec((4, 2, ROWS, TILE), lambda j: (0, 0, 0, j))
    shape = lambda t: jax.ShapeDtypeStruct((4, 2, ROWS, A_COLS), t)
    return hidden_call(
        x_first_kernel, 0, A_COLS // TILE, scaled, weights, [spec] * 2, [shape(F32), shape(BF)], "hidden_x_first"
    )


def y_first(scaled, weights):
    both = pl.BlockSpec((2, 2 * ROWS, TILE), lambda j: (0, 0, j))
    one = pl.BlockSpec((2 * ROWS, TILE), lambda j: (0, j))
    shapes = [jax.ShapeDtypeStruct((2, 2 * ROWS, B_COLS), F32)] * 3 + [jax.ShapeDtypeStruct((2 * ROWS, B_COLS), BF)] * 2
    return hidden_call(
        y_first_kernel,
        A_COLS // TILE,
        B_COLS // TILE,
        scaled,
        weights,
        [both] * 3 + [one] * 2,
        shapes,
        "hidden_y_first",
    )


def y_sums(here, up, down, far_gate, far_up):
    from_below = over_batch(far_gate, 0, 1)
    from_above = over_batch(far_up, 0, -1)
    to_above = jnp.stack([(up[0] + from_below.astype(F32)).astype(BF), up[1].astype(BF)])
    to_below = jnp.stack([down[0].astype(BF), (down[1] + from_above.astype(F32)).astype(BF)])
    below = over_batch(to_above, 0, 1)
    above = over_batch(to_below, 0, -1)
    return here + below.astype(F32) + above.astype(F32)


def on_device(
    queries,
    new_key,
    new_value,
    prefix_keys,
    prefix_values,
    suffix_keys,
    suffix_values,
    suffix_lengths,
    out_weight,
    residual,
    norm_gain,
    gate_weight,
    up_weight,
):
    c = lax.axis_index("ctx")
    b = lax.axis_index("batch")
    xh, z = c // 4, c % 4
    xl, y, core = b // 8, b // 2 % 4, b % 2

    q_across = over_ctx(queries, 1, 0)
    suffix_out, suffix_lse = suffix_part(queries, suffix_keys, suffix_values, new_key, new_value, suffix_lengths)
    q2 = jnp.stack([queries, q_across])
    arrived = {s: over_ctx(q2, 0, s) for s in (1, 3, 2)}

    def groups(from_z):
        return jnp.stack([xh * 4 + from_z, (1 - xh) * 4 + from_z]).astype(jnp.int32)

    own, across = prefix_pair(groups(z), q2, prefix_keys, prefix_values)
    parts = [own, over_ctx(across, 1, 0)]
    for s in (1, 3, 2):
        same, other = prefix_pair(groups((z - s) % 4), arrived[s], prefix_keys, prefix_values)
        parts += [over_ctx(same, 0, -s), over_ctx(other, 1, -s)]
    attended = merge_parts(parts, suffix_out, suffix_lse)

    other_out = over_batch(out_weight, 0, 0, 1)
    other_gate = over_batch(gate_weight, 0, 0, 1)
    other_up = over_batch(up_weight, 0, 0, 1)
    blocks = residual.reshape(4, 2, 2, ROWS, HALF)
    take = lambda k: lax.dynamic_slice(blocks, (z, 0, k, 0, 0), (1, 2, 1, ROWS, HALF)).reshape(96, HALF)
    other_residual = over_batch(take(1 - core), 0, 0, 1)
    own_residual = take(core)

    everyone = lax.all_to_all(
        jnp.broadcast_to(attended[None], (8, ROWS, 1024)),
        "batch",
        0,
        0,
        axis_index_groups=[list(range(0, 16, 2)), list(range(1, 16, 2))],
        tiled=True,
    ).reshape(384, 1024)
    mine, *send = project(z.astype(jnp.int32).reshape(1), everyone, out_weight, other_out)
    for s in (1, 3, 2):
        mine = mine + over_ctx(send[s - 1], 0, s).astype(F32)
    mine = mine.astype(BF)
    across = over_ctx(mine, 1, 0)
    mixed = mine.astype(F32) + across.astype(F32)
    chunk = (jnp.concatenate([own_residual, other_residual], axis=1).astype(F32) + mixed).astype(BF)
    pieces = [chunk] + [over_ctx(chunk, 0, s) for s in (1, 3, 2)]
    piece_z = [z, (z - 1) % 4, (z - 3) % 4, (z - 2) % 4]

    place = []
    for pz in piece_z:
        for e in range(2):
            block = 2 * pz + e
            place.append((block // 4 - xl) % 2 * 4 + (block % 4 - y) % 4)
    gain = jnp.concatenate([norm_gain, over_batch(norm_gain, 0, 0, 1)]).astype(F32).reshape(1, 2 * HALF)
    scaled, squares = fill(jnp.stack(place).astype(jnp.int32), pieces, gain)
    weights = (gate_weight, other_gate, up_weight, other_up)
    keep, send = x_first(scaled, weights)
    here, up, down, far_gate, far_up = y_first(scaled, weights)

    got = over_batch(send, 1, 0)
    total = lambda k: keep[k] + got[k].astype(F32)
    far = total(2).astype(BF)
    a_sums = y_sums(total(0), total(1), total(3), far[0], far[1])
    b_sums = y_sums(here, up, down, far_gate, far_up)
    b_sums = b_sums[:, :ROWS] + over_batch(b_sums[:, ROWS:].astype(BF), 1, 0).astype(F32)

    squares = squares[:, 0].reshape(2, 4, ROWS)
    squares = squares[0] + over_batch(squares[1], 1, 0)
    square_sums = squares[0]
    for s in (1, 2, 3):
        square_sums = square_sums + over_batch(squares[s], 0, s)
    rms = jnp.sqrt(square_sums / D + 1e-05)[:, None]

    def activate(sums):
        return (jax.nn.silu(sums[0] / rms) * (sums[1] / rms)).astype(BF)

    activation = jnp.concatenate([activate(a_sums), activate(b_sums)], axis=1)

    theirs = [over_batch(jnp.concatenate([p[:, HALF:] for p in pieces]), 0, 0, 1)]
    ordered = jnp.stack(
        [jnp.concatenate([p[:, :HALF] for p in pieces]).reshape(4, 2, ROWS, HALF), theirs[0].reshape(4, 2, ROWS, HALF)]
    )
    ordered = jnp.where(core == 0, ordered, ordered[::-1])
    stream = jnp.zeros((4, 2, 2, ROWS, HALF), BF)
    for j, pz in enumerate(piece_z):
        stream = lax.dynamic_update_slice(stream, ordered[:, j].transpose(1, 0, 2, 3)[None], (pz, 0, 0, 0, 0))
    return (stream.reshape(768, HALF), activation)


def solution(mesh):
    in_specs = (
        P("batch", "ctx"),
        P("batch", "ctx"),
        P("batch", "ctx"),
        P("ctx", None),
        P("ctx", None),
        P("batch", None, "ctx"),
        P("batch", None, "ctx"),
        P("batch"),
        P("ctx", "batch"),
        P(None, "batch"),
        P("batch"),
        P("batch", "ctx"),
        P("batch", "ctx"),
    )
    out_specs = (P(None, "batch"), P("batch", "ctx"))
    return jax.shard_map(
        on_device, mesh=mesh, in_specs=in_specs, out_specs=out_specs, check_vma=False
    )
```

```python
import functools

import jax
import jax.numpy as jnp
from jax import lax
from jax.experimental import pallas as pl
from jax.experimental.pallas import tpu as pltpu
from jax.sharding import PartitionSpec as P

D = 8192
KV = 8
HD = 128
SUF = 128
GROUP = 8
ROWS = 48
QROWS = ROWS * GROUP
META = 16
PAYLOAD = QROWS + QROWS // 128 * META
PRE = 2048
HALF = 512
HIDDEN = 3584
A_COLS = 1280
B_COLS = HIDDEN - A_COLS
A_TILE = 256
B_TILE = 768
SAME_CORE = [list(range(0, 16, 2)), list(range(1, 16, 2))]
BF = jnp.bfloat16
F32 = jnp.float32
VMEM = 16 << 20
Q_TILE = 192
LOG2E = 1.4426950408889634


def ctx_perm(flip, s):
    return [(x * 4 + z, (x ^ flip) * 4 + (z + s) % 4) for x in range(2) for z in range(4)]


def batch_perm(flip_x, s, flip_core):
    return [
        (x * 8 + y * 2 + k, (x ^ flip_x) * 8 + (y + s) % 4 * 2 + (k ^ flip_core))
        for x in range(2)
        for y in range(4)
        for k in range(2)
    ]


def over_ctx(v, flip, s):
    return lax.ppermute(v, "ctx", ctx_perm(flip, s))


def over_batch(v, flip_x, s, flip_core=0):
    return lax.ppermute(v, "batch", batch_perm(flip_x, s, flip_core))


def nt_dot(a, b):
    return lax.dot_general(a, b, (((1,), (1,)), ((), ())), preferred_element_type=F32)


def heads_as_rows(q):
    return jnp.concatenate([q[:, h * HD : (h + 1) * HD] for h in range(GROUP)], axis=0)


def split3(v):
    hi = v.astype(BF).astype(F32)
    rest = v - hi
    mid = rest.astype(BF).astype(F32)
    return hi, mid, rest - mid


def attend_prefix(q, k, v):
    scale = 1.0 / (HD**0.5)
    outs, sums = [], []
    for t in range(QROWS // Q_TILE):
        s = nt_dot(q[t * Q_TILE : (t + 1) * Q_TILE], k)
        top = jnp.max(s, axis=1, keepdims=True)
        w = jnp.exp2((s - top) * (scale * LOG2E))
        total = jnp.sum(w, axis=1, keepdims=True)
        o = jnp.dot(w.astype(BF), v, preferred_element_type=F32)
        outs.append((o / total).astype(BF))
        sums.append(top * scale + jnp.log(total))
    return outs, jnp.concatenate(sums, axis=0)


def put_payload(put, outs, lse):
    column = lax.broadcasted_iota(jnp.int32, (128, 128), 1)
    for t, o in enumerate(outs):
        put(t * Q_TILE, o)
    for t in range(QROWS // 128):
        hi, mid, lo = split3(lse[t * 128 : (t + 1) * 128])
        parts = jnp.where(column == 0, hi, jnp.where(column == 1, mid, jnp.where(column == 2, lo, 0.0)))
        put(QROWS + t * META, parts.T[:META].astype(BF))


def prefix_kernel(which, group_ref, q_ref, k_ref, v_ref, *refs):
    out_ref = refs[-1]
    at = pl.ds(pl.multiple_of(group_ref[0] * HD, HD), HD)
    q = heads_as_rows(q_ref[...] if which is None else q_ref[which])

    def put(row, value):
        out_ref[row : row + value.shape[0], :] = value

    put_payload(put, *attend_prefix(q, k_ref[:, at], v_ref[:, at]))


def prefix_part(group, q, which, keys, values, after):
    vmem = pl.BlockSpec(memory_space=pltpu.VMEM)
    return pl.pallas_call(
        functools.partial(prefix_kernel, which),
        in_specs=[pl.BlockSpec(memory_space=pltpu.SMEM), pl.BlockSpec(), vmem, vmem]
        + [pl.BlockSpec(memory_space=pl.ANY)] * len(after),
        out_shape=jax.ShapeDtypeStruct((PAYLOAD, HD), BF),
        compiler_params=pltpu.CompilerParams(vmem_limit_bytes=VMEM),
        cost_estimate=pl.CostEstimate(
            flops=4 * QROWS * PRE * HD, bytes_accessed=2 * 2 * PRE * HD, transcendentals=QROWS * PRE
        ),
        name="prefix_part",
    )(group.astype(jnp.int32).reshape(1), q, keys, values, *after)


def pair_kernel(mine_ref, across_ref, _, out_ref):
    out_ref[0] = mine_ref[...]
    out_ref[1] = across_ref[...]


def pair_up(mine, across, after):
    return pl.pallas_call(
        pair_kernel,
        in_specs=[pl.BlockSpec(), pl.BlockSpec(), pl.BlockSpec(memory_space=pl.ANY)],
        out_shape=jax.ShapeDtypeStruct((2, *mine.shape), mine.dtype),
        compiler_params=pltpu.CompilerParams(vmem_limit_bytes=VMEM),
        cost_estimate=pl.CostEstimate(flops=0, bytes_accessed=4 * mine.size * 2, transcendentals=0),
        name="pair_up",
    )(mine, across, after)


SUF_LEAVES = 16


def suffix_kernel(q_ref, k_ref, v_ref, nk_ref, nv_ref, len_ref, o_ref, lse_ref):
    scale = 1.0 / (HD**0.5)
    n = SUF_LEAVES * GROUP
    q = heads_as_rows(q_ref[...])
    s = nt_dot(q, k_ref[...]) * scale
    lengths = jnp.concatenate([len_ref[...][:, :1]] * GROUP, axis=0)
    row = lax.broadcasted_iota(jnp.int32, (n, 1), 0) % SUF_LEAVES
    slot = lax.broadcasted_iota(jnp.int32, s.shape, 1) - row * SUF
    s = jnp.where((slot >= 0) & (slot < lengths), s, -1e30)
    fresh_key = jnp.concatenate([nk_ref[...].astype(F32)] * GROUP, axis=0)
    fresh = jnp.sum(q.astype(F32) * fresh_key, axis=1, keepdims=True) * scale
    top = jnp.maximum(jnp.max(s, axis=1, keepdims=True), fresh)
    w = jnp.exp(s - top)
    wn = jnp.exp(fresh - top)
    total = jnp.sum(w, axis=1, keepdims=True) + wn
    o = jnp.dot(w.astype(BF), v_ref[...], preferred_element_type=F32)
    fresh_value = jnp.concatenate([nv_ref[...].astype(F32)] * GROUP, axis=0)
    o = (o + wn.astype(BF).astype(F32) * fresh_value) / total
    lse = jnp.broadcast_to(top + jnp.log(total), o.shape)
    for h in range(GROUP):
        o_ref[h] = o[h * SUF_LEAVES : (h + 1) * SUF_LEAVES]
        lse_ref[h] = lse[h * SUF_LEAVES : (h + 1) * SUF_LEAVES]


def suffix_part(q, keys, values, new_key, new_value, lengths):
    shape = jax.ShapeDtypeStruct((GROUP, ROWS, HD), F32)
    leaf = lambda w: pl.BlockSpec((SUF_LEAVES, w), lambda i: (i, 0))
    cached = pl.BlockSpec((SUF_LEAVES * SUF, HD), lambda i: (i, 0))
    return pl.pallas_call(
        suffix_kernel,
        grid=(ROWS // SUF_LEAVES,),
        in_specs=[leaf(GROUP * HD), cached, cached, leaf(HD), leaf(HD), leaf(HD)],
        out_specs=[pl.BlockSpec((GROUP, SUF_LEAVES, HD), lambda i: (0, i, 0))] * 2,
        out_shape=[shape, shape],
        compiler_params=pltpu.CompilerParams(vmem_limit_bytes=VMEM),
        cost_estimate=pl.CostEstimate(flops=4 * QROWS * 2048 * HD, bytes_accessed=4 << 20, transcendentals=QROWS * 2048),
        name="suffix_part",
    )(
        q,
        keys.reshape(ROWS * SUF, HD),
        values.reshape(ROWS * SUF, HD),
        new_key,
        new_value,
        jnp.broadcast_to(lengths[:, None], (ROWS, HD)),
    )


def merge_kernel(*refs):
    parts, (so_ref, sl_ref, out_ref, token_ref, held) = refs[:KV], refs[KV:]
    token_ref[...] = jnp.zeros_like(token_ref)

    def rows_of(at, n):
        return [p[at : at + n, :].astype(F32) for p in parts]

    for t in range(QROWS // 128):
        rows = [m[0:1] + m[1:2] + m[2:3] for m in rows_of(QROWS + t * META, META)]
        lse = jnp.concatenate(rows, axis=0).T
        suf_lse = sl_ref[t * 128 : (t + 1) * 128, :1]
        top = jnp.maximum(jnp.max(lse, axis=1, keepdims=True), suf_lse)
        w = jnp.exp(lse - top)
        ws = jnp.exp(suf_lse - top)
        total = jnp.sum(w, axis=1, keepdims=True) + ws
        o = so_ref[t * 128 : (t + 1) * 128, :] * ws
        for i, p in enumerate(rows_of(t * 128, 128)):
            o = o + p * w[:, i : i + 1]
        held[t * 128 : (t + 1) * 128, :] = (o / total).astype(BF)
    for n in range(8):
        for h in range(GROUP):
            out_ref[n, :, h * HD : (h + 1) * HD] = held[h * ROWS : (h + 1) * ROWS, :]


def merge_parts(parts, suffix_out, suffix_lse):
    return pl.pallas_call(
        merge_kernel,
        out_shape=[jax.ShapeDtypeStruct((8, ROWS, GROUP * HD), BF), jax.ShapeDtypeStruct((8, HD), F32)],
        scratch_shapes=[pltpu.VMEM((QROWS, HD), BF)],
        compiler_params=pltpu.CompilerParams(vmem_limit_bytes=VMEM),
        cost_estimate=pl.CostEstimate(flops=QROWS * HD * 20, bytes_accessed=2 << 20, transcendentals=QROWS * 10),
        name="merge_parts",
    )(*parts, suffix_out.reshape(QROWS, HD), suffix_lse.reshape(QROWS, HD))


def project_kernel(z_ref, a_ref, own_w_ref, other_w_ref, g0_ref, g1_ref, _, gain_ref, mine_ref, *send_refs):
    gain_ref[:, :HALF] = g0_ref[...].astype(F32)
    gain_ref[:, HALF:] = g1_ref[...].astype(F32)
    z = z_ref[0]
    pieces = [a_ref[pl.ds(pl.multiple_of((z + s) % 4 * 96, 16), 96), :] for s in range(4)]
    a = jnp.concatenate(pieces, axis=0)
    for half, w_ref in enumerate((own_w_ref, other_w_ref)):
        y = jnp.dot(a, w_ref[...], preferred_element_type=F32)
        at = slice(half * HALF, (half + 1) * HALF)
        mine_ref[:, at] = y[:96]
        for s, ref in enumerate(send_refs):
            ref[:, at] = y[(s + 1) * 96 : (s + 2) * 96].astype(BF)


def project(z, attended, own_w, other_w, own_gain, other_gain, token):
    vmem = pl.BlockSpec(memory_space=pltpu.VMEM)
    return pl.pallas_call(
        project_kernel,
        in_specs=[pl.BlockSpec(memory_space=pltpu.SMEM)] + [vmem] * 5 + [pl.BlockSpec(memory_space=pl.ANY)],
        out_specs=[vmem] * 5,
        out_shape=[jax.ShapeDtypeStruct((1, 2 * HALF), F32), jax.ShapeDtypeStruct((96, 2 * HALF), F32)] + [jax.ShapeDtypeStruct((96, 2 * HALF), BF)] * 3,
        compiler_params=pltpu.CompilerParams(vmem_limit_bytes=VMEM),
        cost_estimate=pl.CostEstimate(flops=2 * 384 * 1024 * 1024, bytes_accessed=4 << 20, transcendentals=0),
        name="project",
    )(z, attended, own_w, other_w, own_gain, other_gain, token)


def fill_kernel(place_ref, *refs):
    pieces, (gain_ref, scaled_ref, squares_ref, theirs_ref) = refs[:4], refs[4:]
    for j, piece in enumerate(pieces):
        for e in range(2):
            sent = pl.multiple_of(place_ref[j * 2 + e] * ROWS, 16)
            block = pl.multiple_of(place_ref[8 + j * 2 + e] * ROWS, 16)
            rows = piece[e * ROWS : (e + 1) * ROWS, :]
            wide = rows.astype(F32)
            scaled_ref[pl.ds(sent, ROWS), :] = (wide * gain_ref[...]).astype(BF)
            theirs_ref[pl.ds(block, ROWS), :] = rows[:, HALF:]
            squares = jnp.sum(wide * wide, axis=1, keepdims=True)
            squares_ref[pl.ds(sent, ROWS), :] = jnp.broadcast_to(squares, (ROWS, HD))


def fill(place, pieces, gain):
    vmem = pl.BlockSpec(memory_space=pltpu.VMEM)
    return pl.pallas_call(
        fill_kernel,
        in_specs=[pl.BlockSpec(memory_space=pltpu.SMEM)] + [vmem] * 5,
        out_shape=[
            jax.ShapeDtypeStruct((384, 2 * HALF), BF),
            jax.ShapeDtypeStruct((384, HD), F32),
            jax.ShapeDtypeStruct((384, HALF), BF),
        ],
        compiler_params=pltpu.CompilerParams(vmem_limit_bytes=VMEM),
        cost_estimate=pl.CostEstimate(flops=384 * 4096, bytes_accessed=2 << 20, transcendentals=0),
        name="scale_rows",
    )(place, *pieces, gain)


def assemble_kernel(place_ref, *refs):
    pieces, (theirs_ref, out_ref) = refs[:4], refs[4:]
    core = place_ref[16]
    for j, piece in enumerate(pieces):
        for e in range(2):
            block = place_ref[8 + j * 2 + e]
            ours = pl.multiple_of((block * 2 + core) * ROWS, 16)
            other = pl.multiple_of((block * 2 + 1 - core) * ROWS, 16)
            out_ref[pl.ds(ours, ROWS), :] = piece[e * ROWS : (e + 1) * ROWS, :HALF]
            out_ref[pl.ds(other, ROWS), :] = theirs_ref[pl.ds(pl.multiple_of(block * ROWS, 16), ROWS), :]


def assemble(place, pieces, theirs):
    return pl.pallas_call(
        assemble_kernel,
        in_specs=[pl.BlockSpec(memory_space=pltpu.SMEM)] + [pl.BlockSpec()] * 5,
        out_shape=jax.ShapeDtypeStruct((768, HALF), BF),
        compiler_params=pltpu.CompilerParams(vmem_limit_bytes=VMEM),
        cost_estimate=pl.CostEstimate(flops=0, bytes_accessed=2 << 20, transcendentals=0),
        name="assemble_stream",
    )(place, *pieces, theirs)


def weight_tiles(first, columns, tile, weights, held, sems):
    copies = []
    tiles = columns // tile
    for t in range(tiles):
        at = slice(first + t * tile, first + (t + 1) * tile)
        copies.append([pltpu.make_async_copy(w.at[:, at], held.at[t, i], sems.at[t, i]) for i, w in enumerate(weights)])
        for copy in copies[t]:
            copy.start()
    for t in range(tiles):
        for copy in copies[t]:
            copy.wait()
        yield t, [held[t, i] for i in range(4)]


def hidden_sums(s, own_gate, other_gate, own_up, other_up):
    out = []
    for own, other in ((own_gate, other_gate), (own_up, other_up)):
        y = jnp.dot(s[:, :HALF], own, preferred_element_type=F32)
        out.append(y + jnp.dot(s[:, HALF:], other, preferred_element_type=F32))
    return out


def x_first_kernel(first, columns, s_ref, g0, g1, u0, u1, *refs):
    keep_ref, send_ref, held, sems = refs[-4:]
    for t, blocks in weight_tiles(first, columns, A_TILE, (g0, g1, u0, u1), held, sems):
        to = slice(t * A_TILE, (t + 1) * A_TILE)
        for n, y in enumerate(hidden_sums(s_ref[...], *blocks)):
            for k in range(4):
                keep_ref[k, n, :, to] = y[k * ROWS : (k + 1) * ROWS].astype(BF)
                send_ref[k, n, :, to] = y[(4 + k) * ROWS : (5 + k) * ROWS].astype(BF)


def y_first_kernel(first, columns, s_ref, g0, g1, u0, u1, squares_ref, *refs):
    here_ref, up_add, up_pass, down_add, down_pass, far_gate, far_up, held, sems = refs
    up, down, far = (up_add, up_pass), (down_pass, down_add), (far_gate, far_up)

    def put(n, to, y):
        for x in range(2):
            at = slice(x * ROWS, (x + 1) * ROWS)
            part = [y[(x * 4 + k) * ROWS : (x * 4 + k + 1) * ROWS] for k in range(4)]
            here_ref[at, to.start + n * (columns + HD) : to.stop + n * (columns + HD)] = part[0].astype(BF)
            for ref, value in ((up[n], part[1]), (far[n], part[2]), (down[n], part[3])):
                ref[at, to] = value.astype(BF)

    put(0, slice(columns, columns + HD), squares_ref[...])
    for t, blocks in weight_tiles(first, columns, B_TILE, (g0, g1, u0, u1), held, sems):
        for n, y in enumerate(hidden_sums(s_ref[...], *blocks)):
            put(n, slice(t * B_TILE, (t + 1) * B_TILE), y)


def hidden_call(kernel, first, columns, tile, scaled, weights, shapes, flops, name, more):
    tiles = columns // tile
    return pl.pallas_call(
        functools.partial(kernel, first, columns),
        in_specs=[pl.BlockSpec()] + [pl.BlockSpec(memory_space=pl.ANY)] * 4 + [pl.BlockSpec()] * len(more),
        out_shape=shapes,
        scratch_shapes=[pltpu.VMEM((tiles, 4, HALF, tile), BF), pltpu.SemaphoreType.DMA((tiles, 4))],
        compiler_params=pltpu.CompilerParams(vmem_limit_bytes=48 << 20),
        cost_estimate=pl.CostEstimate(flops=flops, bytes_accessed=flops // 1000, transcendentals=0),
        name=name,
    )(scaled, *weights, *more)


def x_first(first, columns, scaled, weights, *after):
    shapes = [jax.ShapeDtypeStruct((4, 2, ROWS, columns), BF)] * 2
    return hidden_call(
        x_first_kernel, first, columns, A_TILE, scaled, weights, shapes, 10**8, "hidden_x_first", after
    )


def y_first(first, columns, scaled, weights, squares):
    gate, rows = columns + HD, 2 * ROWS
    parts = [gate + columns, gate, columns, columns, gate, gate, columns]
    shapes = [jax.ShapeDtypeStruct((rows, n), BF) for n in parts]
    return hidden_call(
        y_first_kernel, first, columns, B_TILE, scaled, weights, shapes, 10**9, "hidden_y_first", (squares,)
    )


def pass_on_kernel(up_add, up_pass, down_add, down_pass, below, above, to_above, to_below):
    gate = up_add.shape[1]
    to_above[:, :gate] = (up_add[...].astype(F32) + below[...].astype(F32)).astype(BF)
    to_above[:, gate:] = up_pass[...]
    to_below[:, :gate] = down_pass[...]
    to_below[:, gate:] = (down_add[...].astype(F32) + above[...].astype(F32)).astype(BF)


def pass_on(*sums):
    shape = jax.ShapeDtypeStruct((2 * ROWS, sums[0].shape[1] + sums[1].shape[1]), BF)
    return pl.pallas_call(
        pass_on_kernel,
        out_shape=[shape, shape],
        compiler_params=pltpu.CompilerParams(vmem_limit_bytes=VMEM),
        cost_estimate=pl.CostEstimate(flops=10**6, bytes_accessed=5 << 20, transcendentals=0),
        name="pass_on_sums",
    )(*sums)


def add_kernel(keep_ref, got_ref, _, __, mine_ref, *send_refs):
    for k, ref in enumerate((mine_ref, *send_refs)):
        ref[...] = (keep_ref[k].astype(F32) + got_ref[k].astype(F32)).astype(ref.dtype)


def add_got(keep, got, after):
    held = pl.BlockSpec(memory_space=pl.ANY)
    return pl.pallas_call(
        add_kernel,
        in_specs=[pl.BlockSpec(), pl.BlockSpec(), held, held],
        out_shape=[jax.ShapeDtypeStruct(keep.shape[1:], t) for t in (F32, BF, BF, BF)],
        compiler_params=pltpu.CompilerParams(vmem_limit_bytes=VMEM),
        cost_estimate=pl.CostEstimate(flops=10**6, bytes_accessed=5 << 20, transcendentals=0),
        name="add_across_x",
    )(keep, got, *after)


def x_then_y(keep, send, after):
    mine, *sends = add_got(keep, over_batch(send, 1, 0), after)
    return mine + sum(over_batch(sends[s - 1], 0, s).astype(F32) for s in (2, 1, 3))


def y_sums(up_add, up_pass, down_add, down_pass, far_gate, far_up):
    from_below = over_batch(far_gate, 0, 1)
    from_above = over_batch(far_up, 0, -1)
    to_above, to_below = pass_on(up_add, up_pass, down_add, down_pass, from_below, from_above)
    return over_batch(to_above, 0, 1), over_batch(to_below, 0, -1)


def on_device(
    queries,
    new_key,
    new_value,
    prefix_keys,
    prefix_values,
    suffix_keys,
    suffix_values,
    suffix_lengths,
    out_weight,
    residual,
    norm_gain,
    gate_weight,
    up_weight,
):
    c = lax.axis_index("ctx")
    b = lax.axis_index("batch")
    xh, z = c // 4, c % 4
    xl, y, core = b // 8, b // 2 % 4, b % 2

    other_out = over_batch(out_weight, 0, 0, 1)
    own_gain = norm_gain.reshape(1, HALF)
    other_gain = over_batch(own_gain, 0, 0, 1)
    blocks = residual.reshape(4, 2, 2, ROWS, HALF)
    take = lambda k: lax.dynamic_slice(blocks, (z, 0, k, 0, 0), (1, 2, 1, ROWS, HALF)).reshape(96, HALF)
    residual_rows = jnp.concatenate([take(core), over_batch(take(1 - core), 0, 0, 1)], axis=1)

    def prefix(flip, s, q, which=None, after=()):
        return prefix_part((xh + flip) % 2 * 4 + (z - s) % 4, q, which, prefix_keys, prefix_values, after)

    q_across = over_ctx(queries, 1, 0)
    own = prefix(0, 0, queries)
    q2 = pair_up(queries, q_across, own)
    arrived = {0: None} | {s: over_ctx(q2, 0, s) for s in (1, 3, 2)}
    across = prefix(1, 0, q_across, None, (own,))
    suffix_out, suffix_lse = suffix_part(queries, suffix_keys, suffix_values, new_key, new_value, suffix_lengths)
    parts, last = [own, over_ctx(across, 1, 0)], across
    for s in (1, 3, 2):
        for flip in (1, 0):
            after = (last,) if len(parts) < 5 else (last, parts[len(parts) - 4])
            last = prefix(flip, s, arrived[s], flip, after)
            parts.append(over_ctx(last, flip, -s))
    attended, token = merge_parts(parts, suffix_out, suffix_lse)
    token, gate_weight, up_weight = lax.optimization_barrier((token, gate_weight, up_weight))
    everyone = lax.all_to_all(
        attended,
        "batch",
        0,
        0,
        axis_index_groups=SAME_CORE,
        tiled=True,
    ).reshape(384, 1024)
    gain, mine, *send = project(
        z.astype(jnp.int32).reshape(1), everyone, out_weight, other_out, own_gain, other_gain, token
    )
    other_gate, other_up = over_batch(gate_weight, 0, 0, 1), over_batch(up_weight, 0, 0, 1)
    for s in (1, 3, 2):
        mine = mine + over_ctx(send[s - 1], 0, s).astype(F32)
    mine = mine.astype(BF)
    across = over_ctx(mine, 1, 0)
    mixed = mine.astype(F32) + across.astype(F32)
    chunk = (residual_rows.astype(F32) + mixed).astype(BF)
    pieces = [chunk] + [over_ctx(chunk, 0, s) for s in (1, 3, 2)]
    piece_z = [z, (z - 1) % 4, (z - 3) % 4, (z - 2) % 4]

    blocks = [2 * pz + e for pz in piece_z for e in range(2)]
    place = [(block // 4 - xl) % 2 * 4 + (block % 4 - y) % 4 for block in blocks] + blocks + [core]
    place, other_gate, other_up = lax.optimization_barrier((jnp.stack(place).astype(jnp.int32), other_gate, other_up))
    scaled, squares, their_columns = fill(place, pieces, gain)
    weights = (gate_weight, other_gate, up_weight, other_up)
    b_first = y_first(A_COLS, B_COLS, scaled, weights, squares)
    a_first = x_first(0, A_COLS, scaled, weights, b_first[-1])
    received = y_sums(*b_first[1:])
    b_sums = b_first[0].astype(F32) + received[0].astype(F32) + received[1].astype(F32)
    b_sums = b_sums[:ROWS] + over_batch(b_sums[ROWS:].astype(BF), 1, 0).astype(F32)
    a_sums = x_then_y(*a_first, received)
    rms = jnp.sqrt(b_sums[:, B_COLS : B_COLS + 1] / D + 1e-05)

    def activate(gate, up):
        return (jax.nn.silu(gate / rms) * (up / rms)).astype(BF)

    activation = jnp.concatenate(
        [activate(a_sums[0], a_sums[1]), activate(b_sums[:, :B_COLS], b_sums[:, B_COLS + HD :])], axis=1
    )
    stream = assemble(place, pieces, over_batch(their_columns, 0, 0, 1))
    return (stream, activation)


def solution(mesh):
    in_specs = (
        P("batch", "ctx"),
        P("batch", "ctx"),
        P("batch", "ctx"),
        P("ctx", None),
        P("ctx", None),
        P("batch", None, "ctx"),
        P("batch", None, "ctx"),
        P("batch"),
        P("ctx", "batch"),
        P(None, "batch"),
        P("batch"),
        P("batch", "ctx"),
        P("batch", "ctx"),
    )
    out_specs = (P(None, "batch"), P("batch", "ctx"))
    return jax.shard_map(
        on_device, mesh=mesh, in_specs=in_specs, out_specs=out_specs, check_vma=False
    )
```

```python
import functools

import jax
import jax.numpy as jnp
from jax import lax
from jax.experimental import pallas as pl
from jax.experimental.pallas import tpu as pltpu
from jax.sharding import PartitionSpec as P

D = 8192
KV = 8
HD = 128
SUF = 128
GROUP = 8
ROWS = 48
QROWS = ROWS * GROUP
META = 16
PAYLOAD = QROWS + QROWS // 128 * META
PRE = 2048
HALF = 512
HIDDEN = 3584
A_COLS = 1536
B_COLS = HIDDEN - A_COLS
A_TILE = 512
B_TILE = 512
SAME_CORE = [list(range(0, 16, 2)), list(range(1, 16, 2))]
BF = jnp.bfloat16
F32 = jnp.float32
VMEM = 16 << 20
Q_TILE = 192
OWN_COPIES = 4
LOG2E = 1.4426950408889634


def ctx_perm(flip, s):
    return [(x * 4 + z, (x ^ flip) * 4 + (z + s) % 4) for x in range(2) for z in range(4)]


def batch_perm(flip_x, s, flip_core):
    return [
        (x * 8 + y * 2 + k, (x ^ flip_x) * 8 + (y + s) % 4 * 2 + (k ^ flip_core))
        for x in range(2)
        for y in range(4)
        for k in range(2)
    ]


def over_ctx(v, flip, s):
    return lax.ppermute(v, "ctx", ctx_perm(flip, s))


def over_batch(v, flip_x, s, flip_core=0):
    return lax.ppermute(v, "batch", batch_perm(flip_x, s, flip_core))


def nt_dot(a, b):
    return lax.dot_general(a, b, (((1,), (1,)), ((), ())), preferred_element_type=F32)


def heads_as_rows(q):
    return jnp.concatenate([q[:, h * HD : (h + 1) * HD] for h in range(GROUP)], axis=0)


def split3(v):
    hi = v.astype(BF).astype(F32)
    rest = v - hi
    mid = rest.astype(BF).astype(F32)
    return hi, mid, rest - mid


def attend_prefix(q, k, v):
    scale = 1.0 / (HD**0.5)
    outs, sums = [], []
    for t in range(QROWS // Q_TILE):
        s = nt_dot(q[t * Q_TILE : (t + 1) * Q_TILE], k)
        top = jnp.max(s, axis=1, keepdims=True)
        w = jnp.exp2((s - top) * (scale * LOG2E))
        total = jnp.sum(w, axis=1, keepdims=True)
        o = jnp.dot(w.astype(BF), v, preferred_element_type=F32)
        outs.append((o / total).astype(BF))
        sums.append(top * scale + jnp.log(total))
    return outs, jnp.concatenate(sums, axis=0)


def put_payload(put, outs, lse):
    column = lax.broadcasted_iota(jnp.int32, (128, 128), 1)
    for t, o in enumerate(outs):
        put(t * Q_TILE, o)
    for t in range(QROWS // 128):
        hi, mid, lo = split3(lse[t * 128 : (t + 1) * 128])
        parts = jnp.where(column == 0, hi, jnp.where(column == 1, mid, jnp.where(column == 2, lo, 0.0)))
        put(QROWS + t * META, parts.T[:META].astype(BF))


def prefix_kernel(which, group_ref, q_ref, k_ref, v_ref, *refs):
    out_ref = refs[-1]
    at = pl.ds(pl.multiple_of(group_ref[0] * HD, HD), HD)
    q = heads_as_rows(q_ref[...] if which is None else q_ref[which])

    def put(row, value):
        out_ref[row : row + value.shape[0], :] = value

    put_payload(put, *attend_prefix(q, k_ref[:, at], v_ref[:, at]))


def own_prefix_kernel(group_ref, q_ref, k_ref, v_ref, out_ref, token_ref, k_held, v_held, sems):
    token_ref[...] = jnp.zeros_like(token_ref)
    at = pl.ds(pl.multiple_of(group_ref[0] * HD, HD), HD)
    copies = []
    for n, (source, held) in enumerate(((k_ref, k_held), (v_ref, v_held))):
        for m in range(OWN_COPIES):
            rows = pl.ds(m * (PRE // OWN_COPIES), PRE // OWN_COPIES)
            copies.append(pltpu.make_async_copy(source.at[rows, at], held.at[rows], sems.at[n, m]))
    for copy in copies:
        copy.start()
    for copy in copies:
        copy.wait()

    def put(row, value):
        out_ref[row : row + value.shape[0], :] = value

    put_payload(put, *attend_prefix(heads_as_rows(q_ref[...]), k_held[...], v_held[...]))


def own_prefix(group, q, keys, values):
    held = pl.BlockSpec(memory_space=pl.ANY)
    return pl.pallas_call(
        own_prefix_kernel,
        in_specs=[pl.BlockSpec(memory_space=pltpu.SMEM), pl.BlockSpec(), held, held],
        out_shape=[jax.ShapeDtypeStruct((PAYLOAD, HD), BF), jax.ShapeDtypeStruct((8, HD), F32)],
        scratch_shapes=[pltpu.VMEM((PRE, HD), BF), pltpu.VMEM((PRE, HD), BF), pltpu.SemaphoreType.DMA((2, OWN_COPIES))],
        compiler_params=pltpu.CompilerParams(vmem_limit_bytes=59 << 20),
        cost_estimate=pl.CostEstimate(
            flops=4 * QROWS * PRE * HD, bytes_accessed=2 * 2 * PRE * HD, transcendentals=QROWS * PRE
        ),
        name="own_prefix",
    )(group, q, keys, values)


def prefix_part(group, q, which, keys, values, after):
    vmem = pl.BlockSpec(memory_space=pltpu.VMEM)
    return pl.pallas_call(
        functools.partial(prefix_kernel, which),
        in_specs=[pl.BlockSpec(memory_space=pltpu.SMEM), pl.BlockSpec(), vmem, vmem]
        + [pl.BlockSpec(memory_space=pl.ANY)] * len(after),
        out_shape=jax.ShapeDtypeStruct((PAYLOAD, HD), BF),
        compiler_params=pltpu.CompilerParams(vmem_limit_bytes=VMEM),
        cost_estimate=pl.CostEstimate(
            flops=4 * QROWS * PRE * HD, bytes_accessed=2 * 2 * PRE * HD, transcendentals=QROWS * PRE
        ),
        name="prefix_part",
    )(group, q, keys, values, *after)


def pair_kernel(mine_ref, across_ref, _, out_ref):
    out_ref[0] = mine_ref[...]
    out_ref[1] = across_ref[...]


def pair_up(mine, across, after):
    return pl.pallas_call(
        pair_kernel,
        out_shape=jax.ShapeDtypeStruct((2, *mine.shape), mine.dtype),
        compiler_params=pltpu.CompilerParams(vmem_limit_bytes=VMEM),
        cost_estimate=pl.CostEstimate(flops=0, bytes_accessed=4 * mine.size * 2, transcendentals=0),
        name="pair_up",
    )(mine, across, after)


SUF_LEAVES = 16


def suffix_kernel(q_ref, k_ref, v_ref, nk_ref, nv_ref, len_ref, o_ref, lse_ref):
    scale = 1.0 / (HD**0.5)
    n = SUF_LEAVES * GROUP
    q = heads_as_rows(q_ref[...])
    s = nt_dot(q, k_ref[...]) * scale
    lengths = jnp.concatenate([len_ref[...][:, :1]] * GROUP, axis=0)
    row = lax.broadcasted_iota(jnp.int32, (n, 1), 0) % SUF_LEAVES
    slot = lax.broadcasted_iota(jnp.int32, s.shape, 1) - row * SUF
    s = jnp.where((slot >= 0) & (slot < lengths), s, -1e30)
    fresh_key = jnp.concatenate([nk_ref[...].astype(F32)] * GROUP, axis=0)
    fresh = jnp.sum(q.astype(F32) * fresh_key, axis=1, keepdims=True) * scale
    top = jnp.maximum(jnp.max(s, axis=1, keepdims=True), fresh)
    w = jnp.exp(s - top)
    wn = jnp.exp(fresh - top)
    total = jnp.sum(w, axis=1, keepdims=True) + wn
    o = jnp.dot(w.astype(BF), v_ref[...], preferred_element_type=F32)
    fresh_value = jnp.concatenate([nv_ref[...].astype(F32)] * GROUP, axis=0)
    o = (o + wn.astype(BF).astype(F32) * fresh_value) / total
    lse = jnp.broadcast_to(top + jnp.log(total), o.shape)
    for h in range(GROUP):
        o_ref[h] = o[h * SUF_LEAVES : (h + 1) * SUF_LEAVES]
        lse_ref[h] = lse[h * SUF_LEAVES : (h + 1) * SUF_LEAVES]


def suffix_part(q, keys, values, new_key, new_value, lengths):
    shape = jax.ShapeDtypeStruct((GROUP, ROWS, HD), F32)
    leaf = lambda w: pl.BlockSpec((SUF_LEAVES, w), lambda i: (i, 0))
    cached = pl.BlockSpec((SUF_LEAVES * SUF, HD), lambda i: (i, 0))
    return pl.pallas_call(
        suffix_kernel,
        grid=(ROWS // SUF_LEAVES,),
        in_specs=[leaf(GROUP * HD), cached, cached, leaf(HD), leaf(HD), leaf(HD)],
        out_specs=[pl.BlockSpec((GROUP, SUF_LEAVES, HD), lambda i: (0, i, 0))] * 2,
        out_shape=[shape, shape],
        compiler_params=pltpu.CompilerParams(vmem_limit_bytes=VMEM),
        cost_estimate=pl.CostEstimate(flops=4 * QROWS * 2048 * HD, bytes_accessed=4 << 20, transcendentals=QROWS * 2048),
        name="suffix_part",
    )(
        q,
        keys.reshape(ROWS * SUF, HD),
        values.reshape(ROWS * SUF, HD),
        new_key,
        new_value,
        jnp.broadcast_to(lengths[:, None], (ROWS, HD)),
    )


def merge_kernel(*refs):
    parts, (so_ref, sl_ref, out_ref, held) = refs[:KV], refs[KV:]

    def rows_of(at, n):
        return [p[at : at + n, :].astype(F32) for p in parts]

    for t in range(QROWS // 128):
        rows = [m[0:1] + m[1:2] + m[2:3] for m in rows_of(QROWS + t * META, META)]
        lse = jnp.concatenate(rows, axis=0).T
        suf_lse = sl_ref[t * 128 : (t + 1) * 128, :1]
        top = jnp.maximum(jnp.max(lse, axis=1, keepdims=True), suf_lse)
        w = jnp.exp(lse - top)
        ws = jnp.exp(suf_lse - top)
        total = jnp.sum(w, axis=1, keepdims=True) + ws
        o = so_ref[t * 128 : (t + 1) * 128, :] * ws
        for i, p in enumerate(rows_of(t * 128, 128)):
            o = o + p * w[:, i : i + 1]
        held[t * 128 : (t + 1) * 128, :] = (o / total).astype(BF)
    for n in range(8):
        for h in range(GROUP):
            out_ref[n, :, h * HD : (h + 1) * HD] = held[h * ROWS : (h + 1) * ROWS, :]


def merge_parts(parts, suffix_out, suffix_lse):
    return pl.pallas_call(
        merge_kernel,
        out_shape=jax.ShapeDtypeStruct((8, ROWS, GROUP * HD), BF),
        scratch_shapes=[pltpu.VMEM((QROWS, HD), BF)],
        compiler_params=pltpu.CompilerParams(vmem_limit_bytes=VMEM),
        cost_estimate=pl.CostEstimate(flops=QROWS * HD * 20, bytes_accessed=2 << 20, transcendentals=QROWS * 10),
        name="merge_parts",
    )(*parts, suffix_out.reshape(QROWS, HD), suffix_lse.reshape(QROWS, HD))


def project_kernel(z_ref, a_ref, own_w_ref, other_w_ref, g0_ref, g1_ref, gain_ref, mine_ref, *send_refs):
    gain_ref[:, :HALF] = g0_ref[...].astype(F32)
    gain_ref[:, HALF:] = g1_ref[...].astype(F32)
    z = z_ref[0]
    pieces = [a_ref[pl.ds(pl.multiple_of((z + s) % 4 * 96, 16), 96), :] for s in range(4)]
    a = jnp.concatenate(pieces, axis=0)
    for half, w_ref in enumerate((own_w_ref, other_w_ref)):
        y = jnp.dot(a, w_ref[...], preferred_element_type=F32)
        at = slice(half * HALF, (half + 1) * HALF)
        mine_ref[:, at] = y[:96]
        for s, ref in enumerate(send_refs):
            ref[:, at] = y[(s + 1) * 96 : (s + 2) * 96].astype(BF)


def project(z, attended, own_w, other_w, own_gain, other_gain):
    vmem = pl.BlockSpec(memory_space=pltpu.VMEM)
    return pl.pallas_call(
        project_kernel,
        in_specs=[pl.BlockSpec(memory_space=pltpu.SMEM)] + [vmem] * 5,
        out_specs=[vmem] * 5,
        out_shape=[jax.ShapeDtypeStruct((1, 2 * HALF), F32), jax.ShapeDtypeStruct((96, 2 * HALF), F32)] + [jax.ShapeDtypeStruct((96, 2 * HALF), BF)] * 3,
        compiler_params=pltpu.CompilerParams(vmem_limit_bytes=VMEM),
        cost_estimate=pl.CostEstimate(flops=2 * 384 * 1024 * 1024, bytes_accessed=4 << 20, transcendentals=0),
        name="project",
    )(z, attended, own_w, other_w, own_gain, other_gain)


def fill_kernel(place_ref, *refs):
    pieces, (gain_ref, scaled_ref, squares_ref, theirs_ref) = refs[:4], refs[4:]
    for j, piece in enumerate(pieces):
        for e in range(2):
            sent = pl.multiple_of(place_ref[j * 2 + e] * ROWS, 16)
            block = pl.multiple_of(place_ref[8 + j * 2 + e] * ROWS, 16)
            rows = piece[e * ROWS : (e + 1) * ROWS, :]
            wide = rows.astype(F32)
            scaled_ref[pl.ds(sent, ROWS), :] = (wide * gain_ref[...]).astype(BF)
            theirs_ref[pl.ds(block, ROWS), :] = rows[:, HALF:]
            squares = jnp.sum(wide * wide, axis=1, keepdims=True)
            squares_ref[pl.ds(sent, ROWS), :] = jnp.broadcast_to(squares, (ROWS, HD))


def fill(place, pieces, gain):
    vmem = pl.BlockSpec(memory_space=pltpu.VMEM)
    return pl.pallas_call(
        fill_kernel,
        in_specs=[pl.BlockSpec(memory_space=pltpu.SMEM)] + [vmem] * 5,
        out_shape=[
            jax.ShapeDtypeStruct((384, 2 * HALF), BF),
            jax.ShapeDtypeStruct((384, HD), F32),
            jax.ShapeDtypeStruct((384, HALF), BF),
        ],
        compiler_params=pltpu.CompilerParams(vmem_limit_bytes=VMEM),
        cost_estimate=pl.CostEstimate(flops=384 * 4096, bytes_accessed=2 << 20, transcendentals=0),
        name="scale_rows",
    )(place, *pieces, gain)


def assemble_kernel(place_ref, *refs):
    pieces, (theirs_ref, out_ref, token_ref) = refs[:4], refs[4:]
    token_ref[...] = jnp.zeros_like(token_ref)
    core = place_ref[16]
    for j, piece in enumerate(pieces):
        for e in range(2):
            block = place_ref[8 + j * 2 + e]
            ours = pl.multiple_of((block * 2 + core) * ROWS, 16)
            other = pl.multiple_of((block * 2 + 1 - core) * ROWS, 16)
            out_ref[pl.ds(ours, ROWS), :] = piece[e * ROWS : (e + 1) * ROWS, :HALF]
            out_ref[pl.ds(other, ROWS), :] = theirs_ref[pl.ds(pl.multiple_of(block * ROWS, 16), ROWS), :]


def assemble(place, pieces, theirs):
    return pl.pallas_call(
        assemble_kernel,
        in_specs=[pl.BlockSpec(memory_space=pltpu.SMEM)] + [pl.BlockSpec()] * 5,
        out_shape=[jax.ShapeDtypeStruct((768, HALF), BF), jax.ShapeDtypeStruct((8, HD), F32)],
        compiler_params=pltpu.CompilerParams(vmem_limit_bytes=VMEM),
        cost_estimate=pl.CostEstimate(flops=1000, bytes_accessed=1000, transcendentals=0),
        name="assemble_stream",
    )(place, *pieces, theirs)


def weight_tiles(first, columns, tile, weights, held, sems):
    copies = []
    tiles = columns // tile
    for t in range(tiles):
        at = slice(first + t * tile, first + (t + 1) * tile)
        copies.append([pltpu.make_async_copy(w.at[:, at], held.at[t, i], sems.at[t, i]) for i, w in enumerate(weights)])
        for copy in copies[t]:
            copy.start()
    for t in range(tiles):
        for copy in copies[t]:
            copy.wait()
        yield t, [held[t, i] for i in range(4)]


def hidden_sums(s, own_gate, other_gate, own_up, other_up):
    out = []
    for own, other in ((own_gate, other_gate), (own_up, other_up)):
        y = jnp.dot(s[:, :HALF], own, preferred_element_type=F32)
        out.append(y + jnp.dot(s[:, HALF:], other, preferred_element_type=F32))
    return out


def x_first_kernel(first, columns, s_ref, g0, g1, u0, u1, *refs):
    keep_ref, send_ref, token_ref, held, sems = refs[-5:]
    token_ref[...] = jnp.zeros_like(token_ref)
    for t, blocks in weight_tiles(first, columns, A_TILE, (g0, g1, u0, u1), held, sems):
        to = slice(t * A_TILE, (t + 1) * A_TILE)
        for n, y in enumerate(hidden_sums(s_ref[...], *blocks)):
            for k in range(4):
                keep_ref[k, n, :, to] = y[k * ROWS : (k + 1) * ROWS].astype(BF)
                send_ref[k, n, :, to] = y[(4 + k) * ROWS : (5 + k) * ROWS].astype(BF)


def y_first_kernel(first, columns, s_ref, g0, g1, u0, u1, squares_ref, *refs):
    here_ref, up_add, up_pass, down_add, down_pass, far_gate, far_up, held, sems = refs
    up, down, far = (up_add, up_pass), (down_pass, down_add), (far_gate, far_up)

    def put(n, to, y):
        for x in range(2):
            at = slice(x * ROWS, (x + 1) * ROWS)
            part = [y[(x * 4 + k) * ROWS : (x * 4 + k + 1) * ROWS] for k in range(4)]
            here_ref[at, to.start + n * (columns + HD) : to.stop + n * (columns + HD)] = part[0].astype(BF)
            for ref, value in ((up[n], part[1]), (far[n], part[2]), (down[n], part[3])):
                ref[at, to] = value.astype(BF)

    put(0, slice(columns, columns + HD), squares_ref[...])
    for t, blocks in weight_tiles(first, columns, B_TILE, (g0, g1, u0, u1), held, sems):
        for n, y in enumerate(hidden_sums(s_ref[...], *blocks)):
            put(n, slice(t * B_TILE, (t + 1) * B_TILE), y)


def hidden_call(kernel, first, columns, tile, scaled, weights, shapes, flops, name, more):
    tiles = columns // tile
    return pl.pallas_call(
        functools.partial(kernel, first, columns),
        in_specs=[pl.BlockSpec()] + [pl.BlockSpec(memory_space=pl.ANY)] * 4 + [pl.BlockSpec()] * len(more),
        out_shape=shapes,
        scratch_shapes=[pltpu.VMEM((tiles, 4, HALF, tile), BF), pltpu.SemaphoreType.DMA((tiles, 4))],
        compiler_params=pltpu.CompilerParams(vmem_limit_bytes=48 << 20),
        cost_estimate=pl.CostEstimate(flops=flops, bytes_accessed=flops // 1000, transcendentals=0),
        name=name,
    )(scaled, *weights, *more)


def x_first(first, columns, scaled, weights, *after):
    shapes = [jax.ShapeDtypeStruct((4, 2, ROWS, columns), BF)] * 2 + [jax.ShapeDtypeStruct((8, HD), F32)]
    return hidden_call(
        x_first_kernel, first, columns, A_TILE, scaled, weights, shapes, 10**8, "hidden_x_first", after
    )


def y_first(first, columns, scaled, weights, squares):
    gate, rows = columns + HD, 2 * ROWS
    parts = [gate + columns, gate, columns, columns, gate, gate, columns]
    shapes = [jax.ShapeDtypeStruct((rows, n), BF) for n in parts]
    return hidden_call(
        y_first_kernel, first, columns, B_TILE, scaled, weights, shapes, 10**9, "hidden_y_first", (squares,)
    )


def pass_on_kernel(up_add, up_pass, down_add, down_pass, below, above, _, to_above, to_below):
    gate = up_add.shape[1]
    to_above[:, :gate] = (up_add[...].astype(F32) + below[...].astype(F32)).astype(BF)
    to_above[:, gate:] = up_pass[...]
    to_below[:, :gate] = down_pass[...]
    to_below[:, gate:] = (down_add[...].astype(F32) + above[...].astype(F32)).astype(BF)


def pass_on(*sums):
    shape = jax.ShapeDtypeStruct((2 * ROWS, sums[0].shape[1] + sums[1].shape[1]), BF)
    return pl.pallas_call(
        pass_on_kernel,
        out_shape=[shape, shape],
        compiler_params=pltpu.CompilerParams(vmem_limit_bytes=VMEM),
        cost_estimate=pl.CostEstimate(flops=1000, bytes_accessed=1000, transcendentals=0),
        name="pass_on_sums",
    )(*sums)


def finish_kernel(here_ref, below_ref, above_ref, _, keep_ref, send_ref):
    sums = here_ref[...].astype(F32) + below_ref[...].astype(F32) + above_ref[...].astype(F32)
    keep_ref[...] = sums[:ROWS]
    send_ref[...] = sums[ROWS:].astype(BF)


def finish_y(here, below, above, after):
    shape = lambda t: jax.ShapeDtypeStruct((ROWS, here.shape[1]), t)
    return pl.pallas_call(
        finish_kernel,
        in_specs=[pl.BlockSpec()] * 4,
        out_shape=[shape(F32), shape(BF)],
        compiler_params=pltpu.CompilerParams(vmem_limit_bytes=VMEM),
        cost_estimate=pl.CostEstimate(flops=1000, bytes_accessed=1000, transcendentals=0),
        name="finish_y",
    )(here, below, above, after)


def add_kernel(keep_ref, got_ref, _, mine_ref, *send_refs):
    for k, ref in enumerate((mine_ref, *send_refs)):
        ref[...] = (keep_ref[k].astype(F32) + got_ref[k].astype(F32)).astype(ref.dtype)


def add_got(keep, got, after):
    held = pl.BlockSpec(memory_space=pl.ANY)
    return pl.pallas_call(
        add_kernel,
        in_specs=[pl.BlockSpec(), pl.BlockSpec(), held],
        out_shape=[jax.ShapeDtypeStruct(keep.shape[1:], t) for t in (F32, BF, BF, BF)],
        compiler_params=pltpu.CompilerParams(vmem_limit_bytes=VMEM),
        cost_estimate=pl.CostEstimate(flops=1000, bytes_accessed=1000, transcendentals=0),
        name="add_across_x",
    )(keep, got, after)


def activate(gate, up, rms):
    return (jax.nn.silu(gate / rms) * (up / rms)).astype(BF)


def finish_b_kernel(keep_ref, got_ref, out_ref, rms_ref):
    columns = out_ref.shape[1]
    sums = keep_ref[...] + got_ref[...].astype(F32)
    rms = jnp.sqrt(sums[:, columns : columns + HD] / D + 1e-05)
    rms_ref[...] = rms
    out_ref[...] = activate(sums[:, :columns], sums[:, columns + HD :], rms[:, :1])


def finish_b(keep, got):
    return pl.pallas_call(
        finish_b_kernel,
        out_shape=[jax.ShapeDtypeStruct((ROWS, B_COLS), BF), jax.ShapeDtypeStruct((ROWS, HD), F32)],
        compiler_params=pltpu.CompilerParams(vmem_limit_bytes=VMEM),
        cost_estimate=pl.CostEstimate(flops=10**6, bytes_accessed=1 << 20, transcendentals=10**5),
        name="finish_b",
    )(keep, got)


def finish_a_kernel(mine_ref, *refs):
    got, (b_ref, rms_ref, out_ref) = refs[:3], refs[3:]
    gate, up = (mine_ref[n] + sum(g[n].astype(F32) for g in got) for n in range(2))
    out_ref[:, :A_COLS] = activate(gate, up, rms_ref[:, :1])
    out_ref[:, A_COLS:] = b_ref[...]


def finish_a(mine, got, b_part, rms):
    return pl.pallas_call(
        finish_a_kernel,
        out_shape=jax.ShapeDtypeStruct((ROWS, HIDDEN), BF),
        compiler_params=pltpu.CompilerParams(vmem_limit_bytes=VMEM),
        cost_estimate=pl.CostEstimate(flops=10**6, bytes_accessed=1 << 20, transcendentals=10**5),
        name="finish_a",
    )(mine, *got, b_part, rms)


def y_sums(up_add, up_pass, down_add, down_pass, far_gate, far_up, token):
    from_below = over_batch(far_gate, 0, 1)
    from_above = over_batch(far_up, 0, -1)
    to_above, to_below = pass_on(up_add, up_pass, down_add, down_pass, from_below, from_above, token)
    return over_batch(to_above, 0, 1), over_batch(to_below, 0, -1)


def on_device(
    queries,
    new_key,
    new_value,
    prefix_keys,
    prefix_values,
    suffix_keys,
    suffix_values,
    suffix_lengths,
    out_weight,
    residual,
    norm_gain,
    gate_weight,
    up_weight,
):
    c = lax.axis_index("ctx")
    b = lax.axis_index("batch")
    xh, z = c // 4, c % 4
    xl, y, core = b // 8, b // 2 % 4, b % 2

    other_gate, other_up = over_batch(gate_weight, 0, 0, 1), over_batch(up_weight, 0, 0, 1)
    other_out = over_batch(out_weight, 0, 0, 1)
    own_gain = norm_gain.reshape(1, HALF)
    other_gain = over_batch(own_gain, 0, 0, 1)
    blocks = residual.reshape(4, 2, 2, ROWS, HALF)
    take = lambda k: lax.dynamic_slice(blocks, (z, 0, k, 0, 0), (1, 2, 1, ROWS, HALF)).reshape(96, HALF)
    residual_rows = jnp.concatenate([take(core), over_batch(take(1 - core), 0, 0, 1)], axis=1)

    def group_of(flip, s):
        return ((xh + flip) % 2 * 4 + (z - s) % 4).astype(jnp.int32).reshape(1)

    q_across = over_ctx(queries, 1, 0)
    own, token = own_prefix(group_of(0, 0), queries, prefix_keys, prefix_values)
    q2 = pair_up(queries, q_across, token)
    arrived = {0: None} | {s: over_ctx(q2, 0, s) for s in (1, 3, 2)}
    across = prefix_part(group_of(1, 0), q_across, None, prefix_keys, prefix_values, ())
    suffix_out, suffix_lse = suffix_part(queries, suffix_keys, suffix_values, new_key, new_value, suffix_lengths)
    parts, last = [own, over_ctx(across, 1, 0)], across
    for s in (1, 3, 2):
        for flip in (1, 0):
            after = (last,) if len(parts) < 5 else (last, parts[len(parts) - 4])
            group = group_of(flip, s)
            if len(parts) == 2:
                group, other_gate, other_up = lax.optimization_barrier((group, other_gate, other_up))
            last = prefix_part(group, arrived[s], flip, prefix_keys, prefix_values, after)
            parts.append(over_ctx(last, flip, -s))
    attended = merge_parts(parts, suffix_out, suffix_lse)
    everyone = lax.all_to_all(
        attended,
        "batch",
        0,
        0,
        axis_index_groups=SAME_CORE,
        tiled=True,
    ).reshape(384, 1024)
    gain, mine, *send = project(
        z.astype(jnp.int32).reshape(1), everyone, out_weight, other_out, own_gain, other_gain
    )
    for s in (1, 3, 2):
        mine = mine + over_ctx(send[s - 1], 0, s).astype(F32)
    mine = mine.astype(BF)
    across = over_ctx(mine, 1, 0)
    mixed = mine.astype(F32) + across.astype(F32)
    chunk = (residual_rows.astype(F32) + mixed).astype(BF)
    pieces = [chunk] + [over_ctx(chunk, 0, s) for s in (1, 3, 2)]
    piece_z = [z, (z - 1) % 4, (z - 3) % 4, (z - 2) % 4]

    blocks = [2 * pz + e for pz in piece_z for e in range(2)]
    place = [(block // 4 - xl) % 2 * 4 + (block % 4 - y) % 4 for block in blocks] + blocks + [core]
    place = jnp.stack(place).astype(jnp.int32)
    scaled, squares, their_columns = fill(place, pieces, gain)
    weights = (gate_weight, other_gate, up_weight, other_up)
    b_first = y_first(A_COLS, B_COLS, scaled, weights, squares)
    a_first = x_first(0, A_COLS, scaled, weights, b_first[-1])
    received = y_sums(*b_first[1:], a_first[2])
    stream, token = assemble(place, pieces, over_batch(their_columns, 0, 0, 1))
    b_keep, b_send = finish_y(b_first[0], *received, token)
    b_part, rms = finish_b(b_keep, over_batch(b_send, 1, 0))
    mine, *sends = add_got(a_first[0], over_batch(a_first[1], 1, 0), b_send)
    activation = finish_a(mine, [over_batch(sends[s - 1], 0, s) for s in (2, 1, 3)], b_part, rms)
    return (stream, activation)


def solution(mesh):
    in_specs = (
        P("batch", "ctx"),
        P("batch", "ctx"),
        P("batch", "ctx"),
        P("ctx", None),
        P("ctx", None),
        P("batch", None, "ctx"),
        P("batch", None, "ctx"),
        P("batch"),
        P("ctx", "batch"),
        P(None, "batch"),
        P("batch"),
        P("batch", "ctx"),
        P("batch", "ctx"),
    )
    out_specs = (P(None, "batch"), P("batch", "ctx"))
    return jax.shard_map(
        on_device, mesh=mesh, in_specs=in_specs, out_specs=out_specs, check_vma=False
    )
```

```python
import functools

import jax
import jax.numpy as jnp
from jax import lax
from jax.experimental import pallas as pl
from jax.experimental.pallas import tpu as pltpu
from jax.sharding import PartitionSpec as P

D = 8192
KV = 8
HD = 128
SUF = 128
GROUP = 8
ROWS = 48
QROWS = ROWS * GROUP
META = 16
PAYLOAD = QROWS + QROWS // 128 * META
PRE = 2048
HALF = 512
HIDDEN = 3584
A_COLS = 1408
B_COLS = HIDDEN - A_COLS
TILE = 512
SAME_CORE = [list(range(0, 16, 2)), list(range(1, 16, 2))]
BF = jnp.bfloat16
F32 = jnp.float32
VMEM = 16 << 20
Q_TILE = 192
OWN_COPIES = 4
LOG2E = 1.4426950408889634


def ctx_perm(flip, s):
    return [(x * 4 + z, (x ^ flip) * 4 + (z + s) % 4) for x in range(2) for z in range(4)]


def batch_perm(flip_x, s, flip_core):
    return [
        (x * 8 + y * 2 + k, (x ^ flip_x) * 8 + (y + s) % 4 * 2 + (k ^ flip_core))
        for x in range(2)
        for y in range(4)
        for k in range(2)
    ]


def over_ctx(v, flip, s):
    return lax.ppermute(v, "ctx", ctx_perm(flip, s))


def over_batch(v, flip_x, s, flip_core=0):
    return lax.ppermute(v, "batch", batch_perm(flip_x, s, flip_core))


def nt_dot(a, b):
    return lax.dot_general(a, b, (((1,), (1,)), ((), ())), preferred_element_type=F32)


def heads_as_rows(q):
    return jnp.concatenate([q[:, h * HD : (h + 1) * HD] for h in range(GROUP)], axis=0)


def split3(v):
    hi = v.astype(BF).astype(F32)
    rest = v - hi
    mid = rest.astype(BF).astype(F32)
    return hi, mid, rest - mid


def attend_prefix(q, k, v):
    scale = 1.0 / (HD**0.5)
    outs, sums = [], []
    for t in range(QROWS // Q_TILE):
        s = nt_dot(q[t * Q_TILE : (t + 1) * Q_TILE], k)
        top = jnp.max(s, axis=1, keepdims=True)
        w = jnp.exp2((s - top) * (scale * LOG2E))
        total = jnp.sum(w, axis=1, keepdims=True)
        o = jnp.dot(w.astype(BF), v, preferred_element_type=F32)
        outs.append((o / total).astype(BF))
        sums.append(top * scale + jnp.log(total))
    return outs, jnp.concatenate(sums, axis=0)


def put_payload(put, outs, lse):
    column = lax.broadcasted_iota(jnp.int32, (128, 128), 1)
    for t, o in enumerate(outs):
        put(t * Q_TILE, o)
    for t in range(QROWS // 128):
        hi, mid, lo = split3(lse[t * 128 : (t + 1) * 128])
        parts = jnp.where(column == 0, hi, jnp.where(column == 1, mid, jnp.where(column == 2, lo, 0.0)))
        put(QROWS + t * META, parts.T[:META].astype(BF))


def prefix_kernel(which, group_ref, q_ref, k_ref, v_ref, *refs):
    out_ref = refs[-1]
    at = pl.ds(pl.multiple_of(group_ref[0] * HD, HD), HD)
    q = heads_as_rows(q_ref[...] if which is None else q_ref[which])

    def put(row, value):
        out_ref[row : row + value.shape[0], :] = value

    put_payload(put, *attend_prefix(q, k_ref[:, at], v_ref[:, at]))


def own_prefix_kernel(group_ref, q_ref, k_ref, v_ref, out_ref, token_ref, k_held, v_held, sems):
    token_ref[...] = jnp.zeros_like(token_ref)
    at = pl.ds(pl.multiple_of(group_ref[0] * HD, HD), HD)
    copies = []
    for n, (source, held) in enumerate(((k_ref, k_held), (v_ref, v_held))):
        for m in range(OWN_COPIES):
            rows = pl.ds(m * (PRE // OWN_COPIES), PRE // OWN_COPIES)
            copies.append(pltpu.make_async_copy(source.at[rows, at], held.at[rows], sems.at[n, m]))
    for copy in copies:
        copy.start()
    for copy in copies:
        copy.wait()

    def put(row, value):
        out_ref[row : row + value.shape[0], :] = value

    put_payload(put, *attend_prefix(heads_as_rows(q_ref[...]), k_held[...], v_held[...]))


def own_prefix(group, q, keys, values):
    held = pl.BlockSpec(memory_space=pl.ANY)
    return pl.pallas_call(
        own_prefix_kernel,
        in_specs=[pl.BlockSpec(memory_space=pltpu.SMEM), pl.BlockSpec(), held, held],
        out_shape=[jax.ShapeDtypeStruct((PAYLOAD, HD), BF), jax.ShapeDtypeStruct((8, HD), F32)],
        scratch_shapes=[pltpu.VMEM((PRE, HD), BF), pltpu.VMEM((PRE, HD), BF), pltpu.SemaphoreType.DMA((2, OWN_COPIES))],
        compiler_params=pltpu.CompilerParams(vmem_limit_bytes=59 << 20),
        cost_estimate=pl.CostEstimate(
            flops=4 * QROWS * PRE * HD, bytes_accessed=2 * 2 * PRE * HD, transcendentals=QROWS * PRE
        ),
        name="own_prefix",
    )(group, q, keys, values)


def prefix_part(group, q, which, keys, values, after):
    vmem = pl.BlockSpec(memory_space=pltpu.VMEM)
    return pl.pallas_call(
        functools.partial(prefix_kernel, which),
        in_specs=[pl.BlockSpec(memory_space=pltpu.SMEM), pl.BlockSpec(), vmem, vmem]
        + [pl.BlockSpec(memory_space=pl.ANY)] * len(after),
        out_shape=jax.ShapeDtypeStruct((PAYLOAD, HD), BF),
        compiler_params=pltpu.CompilerParams(vmem_limit_bytes=VMEM),
        cost_estimate=pl.CostEstimate(
            flops=4 * QROWS * PRE * HD, bytes_accessed=2 * 2 * PRE * HD, transcendentals=QROWS * PRE
        ),
        name="prefix_part",
    )(group, q, keys, values, *after)


def pair_kernel(mine_ref, across_ref, _, out_ref):
    out_ref[0] = mine_ref[...]
    out_ref[1] = across_ref[...]


def pair_up(mine, across, after):
    return pl.pallas_call(
        pair_kernel,
        out_shape=jax.ShapeDtypeStruct((2, *mine.shape), mine.dtype),
        compiler_params=pltpu.CompilerParams(vmem_limit_bytes=VMEM),
        cost_estimate=pl.CostEstimate(flops=0, bytes_accessed=4 * mine.size * 2, transcendentals=0),
        name="pair_up",
    )(mine, across, after)


SUF_LEAVES = 16


def suffix_kernel(q_ref, k_ref, v_ref, nk_ref, nv_ref, len_ref, o_ref, lse_ref):
    scale = 1.0 / (HD**0.5)
    n = SUF_LEAVES * GROUP
    q = heads_as_rows(q_ref[...])
    s = nt_dot(q, k_ref[...]) * scale
    lengths = jnp.concatenate([len_ref[...][:, :1]] * GROUP, axis=0)
    row = lax.broadcasted_iota(jnp.int32, (n, 1), 0) % SUF_LEAVES
    slot = lax.broadcasted_iota(jnp.int32, s.shape, 1) - row * SUF
    s = jnp.where((slot >= 0) & (slot < lengths), s, -1e30)
    fresh_key = jnp.concatenate([nk_ref[...].astype(F32)] * GROUP, axis=0)
    fresh = jnp.sum(q.astype(F32) * fresh_key, axis=1, keepdims=True) * scale
    top = jnp.maximum(jnp.max(s, axis=1, keepdims=True), fresh)
    w = jnp.exp(s - top)
    wn = jnp.exp(fresh - top)
    total = jnp.sum(w, axis=1, keepdims=True) + wn
    o = jnp.dot(w.astype(BF), v_ref[...], preferred_element_type=F32)
    fresh_value = jnp.concatenate([nv_ref[...].astype(F32)] * GROUP, axis=0)
    o = (o + wn.astype(BF).astype(F32) * fresh_value) / total
    lse = jnp.broadcast_to(top + jnp.log(total), o.shape)
    for h in range(GROUP):
        o_ref[h] = o[h * SUF_LEAVES : (h + 1) * SUF_LEAVES]
        lse_ref[h] = lse[h * SUF_LEAVES : (h + 1) * SUF_LEAVES]


def suffix_part(q, keys, values, new_key, new_value, lengths):
    shape = jax.ShapeDtypeStruct((GROUP, ROWS, HD), F32)
    leaf = lambda w: pl.BlockSpec((SUF_LEAVES, w), lambda i: (i, 0))
    cached = pl.BlockSpec((SUF_LEAVES * SUF, HD), lambda i: (i, 0))
    return pl.pallas_call(
        suffix_kernel,
        grid=(ROWS // SUF_LEAVES,),
        in_specs=[leaf(GROUP * HD), cached, cached, leaf(HD), leaf(HD), leaf(HD)],
        out_specs=[pl.BlockSpec((GROUP, SUF_LEAVES, HD), lambda i: (0, i, 0))] * 2,
        out_shape=[shape, shape],
        compiler_params=pltpu.CompilerParams(vmem_limit_bytes=VMEM),
        cost_estimate=pl.CostEstimate(flops=4 * QROWS * 2048 * HD, bytes_accessed=4 << 20, transcendentals=QROWS * 2048),
        name="suffix_part",
    )(
        q,
        keys.reshape(ROWS * SUF, HD),
        values.reshape(ROWS * SUF, HD),
        new_key,
        new_value,
        jnp.broadcast_to(lengths[:, None], (ROWS, HD)),
    )


def merge_kernel(*refs):
    parts, (so_ref, sl_ref, out_ref, held) = refs[:KV], refs[KV:]

    def rows_of(at, n):
        return [p[at : at + n, :].astype(F32) for p in parts]

    for t in range(QROWS // 128):
        rows = [m[0:1] + m[1:2] + m[2:3] for m in rows_of(QROWS + t * META, META)]
        lse = jnp.concatenate(rows, axis=0).T
        suf_lse = sl_ref[t * 128 : (t + 1) * 128, :1]
        top = jnp.maximum(jnp.max(lse, axis=1, keepdims=True), suf_lse)
        w = jnp.exp(lse - top)
        ws = jnp.exp(suf_lse - top)
        total = jnp.sum(w, axis=1, keepdims=True) + ws
        o = so_ref[t * 128 : (t + 1) * 128, :] * ws
        for i, p in enumerate(rows_of(t * 128, 128)):
            o = o + p * w[:, i : i + 1]
        held[t * 128 : (t + 1) * 128, :] = (o / total).astype(BF)
    for n in range(8):
        for h in range(GROUP):
            out_ref[n, :, h * HD : (h + 1) * HD] = held[h * ROWS : (h + 1) * ROWS, :]


def merge_parts(parts, suffix_out, suffix_lse):
    return pl.pallas_call(
        merge_kernel,
        out_shape=jax.ShapeDtypeStruct((8, ROWS, GROUP * HD), BF),
        scratch_shapes=[pltpu.VMEM((QROWS, HD), BF)],
        compiler_params=pltpu.CompilerParams(vmem_limit_bytes=VMEM),
        cost_estimate=pl.CostEstimate(flops=QROWS * HD * 20, bytes_accessed=2 << 20, transcendentals=QROWS * 10),
        name="merge_parts",
    )(*parts, suffix_out.reshape(QROWS, HD), suffix_lse.reshape(QROWS, HD))


def project_kernel(z_ref, a_ref, own_w_ref, other_w_ref, g0_ref, g1_ref, gain_ref, mine_ref, *send_refs):
    gain_ref[:, :HALF] = g0_ref[...].astype(F32)
    gain_ref[:, HALF:] = g1_ref[...].astype(F32)
    z = z_ref[0]
    pieces = [a_ref[pl.ds(pl.multiple_of((z + s) % 4 * 96, 16), 96), :] for s in range(4)]
    a = jnp.concatenate(pieces, axis=0)
    for half, w_ref in enumerate((own_w_ref, other_w_ref)):
        y = jnp.dot(a, w_ref[...], preferred_element_type=F32)
        at = slice(half * HALF, (half + 1) * HALF)
        mine_ref[:, at] = y[:96]
        for s, ref in enumerate(send_refs):
            ref[:, at] = y[(s + 1) * 96 : (s + 2) * 96].astype(BF)


def project(z, attended, own_w, other_w, own_gain, other_gain):
    vmem = pl.BlockSpec(memory_space=pltpu.VMEM)
    return pl.pallas_call(
        project_kernel,
        in_specs=[pl.BlockSpec(memory_space=pltpu.SMEM)] + [vmem] * 5,
        out_specs=[vmem] * 5,
        out_shape=[jax.ShapeDtypeStruct((1, 2 * HALF), F32), jax.ShapeDtypeStruct((96, 2 * HALF), F32)] + [jax.ShapeDtypeStruct((96, 2 * HALF), BF)] * 3,
        compiler_params=pltpu.CompilerParams(vmem_limit_bytes=VMEM),
        cost_estimate=pl.CostEstimate(flops=2 * 384 * 1024 * 1024, bytes_accessed=4 << 20, transcendentals=0),
        name="project",
    )(z, attended, own_w, other_w, own_gain, other_gain)


def fill_kernel(place_ref, *refs):
    pieces, (gain_ref, scaled_ref, squares_ref, theirs_ref) = refs[:4], refs[4:]
    for j, piece in enumerate(pieces):
        for e in range(2):
            sent = pl.multiple_of(place_ref[j * 2 + e] * ROWS, 16)
            block = pl.multiple_of(place_ref[8 + j * 2 + e] * ROWS, 16)
            rows = piece[e * ROWS : (e + 1) * ROWS, :]
            wide = rows.astype(F32)
            scaled_ref[pl.ds(sent, ROWS), :] = (wide * gain_ref[...]).astype(BF)
            theirs_ref[pl.ds(block, ROWS), :] = rows[:, HALF:]
            squares = jnp.sum(wide * wide, axis=1, keepdims=True)
            squares_ref[pl.ds(sent, ROWS), :] = jnp.broadcast_to(squares, (ROWS, HD))


def fill(place, pieces, gain):
    vmem = pl.BlockSpec(memory_space=pltpu.VMEM)
    return pl.pallas_call(
        fill_kernel,
        in_specs=[pl.BlockSpec(memory_space=pltpu.SMEM)] + [vmem] * 5,
        out_shape=[
            jax.ShapeDtypeStruct((384, 2 * HALF), BF),
            jax.ShapeDtypeStruct((384, HD), F32),
            jax.ShapeDtypeStruct((384, HALF), BF),
        ],
        compiler_params=pltpu.CompilerParams(vmem_limit_bytes=VMEM),
        cost_estimate=pl.CostEstimate(flops=384 * 4096, bytes_accessed=2 << 20, transcendentals=0),
        name="scale_rows",
    )(place, *pieces, gain)


def assemble_kernel(place_ref, *refs):
    pieces, (theirs_ref, out_ref, token_ref) = refs[:4], refs[4:]
    token_ref[...] = jnp.zeros_like(token_ref)
    core = place_ref[16]
    for j, piece in enumerate(pieces):
        for e in range(2):
            block = place_ref[8 + j * 2 + e]
            ours = pl.multiple_of((block * 2 + core) * ROWS, 16)
            other = pl.multiple_of((block * 2 + 1 - core) * ROWS, 16)
            out_ref[pl.ds(ours, ROWS), :] = piece[e * ROWS : (e + 1) * ROWS, :HALF]
            out_ref[pl.ds(other, ROWS), :] = theirs_ref[pl.ds(pl.multiple_of(block * ROWS, 16), ROWS), :]


def assemble(place, pieces, theirs):
    return pl.pallas_call(
        assemble_kernel,
        in_specs=[pl.BlockSpec(memory_space=pltpu.SMEM)] + [pl.BlockSpec()] * 5,
        out_shape=[jax.ShapeDtypeStruct((768, HALF), BF), jax.ShapeDtypeStruct((8, HD), F32)],
        compiler_params=pltpu.CompilerParams(vmem_limit_bytes=VMEM),
        cost_estimate=pl.CostEstimate(flops=1000, bytes_accessed=1000, transcendentals=0),
        name="assemble_stream",
    )(place, *pieces, theirs)


def hold_kernel(_, *refs):
    sources, places, sems = refs[:4], refs[4:8], refs[8]
    copies = [pltpu.make_async_copy(a, b, sems.at[i]) for i, (a, b) in enumerate(zip(sources, places))]
    for copy in copies:
        copy.start()
    for copy in copies:
        copy.wait()


def hold(after, *arrays):
    return pl.pallas_call(
        hold_kernel,
        in_specs=[pl.BlockSpec()] + [pl.BlockSpec(memory_space=pl.ANY)] * 4,
        out_specs=[pl.BlockSpec(memory_space=pltpu.VMEM)] * 4,
        out_shape=[jax.ShapeDtypeStruct(a.shape, a.dtype) for a in arrays],
        scratch_shapes=[pltpu.SemaphoreType.DMA((4,))],
        compiler_params=pltpu.CompilerParams(vmem_limit_bytes=24 << 20),
        cost_estimate=pl.CostEstimate(flops=0, bytes_accessed=sum(a.size * 4 for a in arrays), transcendentals=0),
        name="hold_weights",
    )(after, *arrays)


def weight_tiles(first, columns, weights):
    ends = range(columns % TILE or TILE, columns + 1, TILE)
    for end in ends:
        at = slice(max(end - TILE, 0), end)
        yield at, [w[:, first + at.start : first + at.stop] for w in weights]


def hidden_sums(s, own_gate, other_gate, own_up, other_up):
    out = []
    for own, other in ((own_gate, other_gate), (own_up, other_up)):
        y = jnp.dot(s[:, :HALF], own, preferred_element_type=F32)
        out.append(y + jnp.dot(s[:, HALF:], other, preferred_element_type=F32))
    return out


def x_first_kernel(first, columns, s_ref, g0, g1, u0, u1, *refs):
    keep_ref, send_ref, token_ref = refs[-3:]
    token_ref[...] = jnp.zeros_like(token_ref)
    for to, blocks in weight_tiles(first, columns, (g0, g1, u0, u1)):
        for n, y in enumerate(hidden_sums(s_ref[...], *blocks)):
            for k in range(4):
                keep_ref[k, n, :, to] = y[k * ROWS : (k + 1) * ROWS].astype(BF)
                send_ref[k, n, :, to] = y[(4 + k) * ROWS : (5 + k) * ROWS].astype(BF)


def y_first_kernel(first, columns, s_ref, g0, g1, u0, u1, squares_ref, *refs):
    here_ref, up_add, up_pass, down_add, down_pass, far_gate, far_up = refs
    up, down, far = (up_add, up_pass), (down_pass, down_add), (far_gate, far_up)

    def put(n, to, y):
        for x in range(2):
            at = slice(x * ROWS, (x + 1) * ROWS)
            part = [y[(x * 4 + k) * ROWS : (x * 4 + k + 1) * ROWS] for k in range(4)]
            here_ref[at, to.start + n * (columns + HD) : to.stop + n * (columns + HD)] = part[0].astype(BF)
            for ref, value in ((up[n], part[1]), (far[n], part[2]), (down[n], part[3])):
                ref[at, to] = value.astype(BF)

    put(0, slice(columns, columns + HD), squares_ref[...])
    for to, blocks in weight_tiles(first, columns, (g0, g1, u0, u1)):
        for n, y in enumerate(hidden_sums(s_ref[...], *blocks)):
            put(n, to, y)


def hidden_call(kernel, first, columns, scaled, weights, shapes, flops, name, more):
    return pl.pallas_call(
        functools.partial(kernel, first, columns),
        in_specs=[pl.BlockSpec()] + [pl.BlockSpec(memory_space=pltpu.VMEM)] * 4 + [pl.BlockSpec()] * len(more),
        out_shape=shapes,
        compiler_params=pltpu.CompilerParams(vmem_limit_bytes=12 << 20),
        cost_estimate=pl.CostEstimate(flops=flops, bytes_accessed=flops // 1000, transcendentals=0),
        name=name,
    )(scaled, *weights, *more)


def x_first(first, columns, scaled, weights, *after):
    shapes = [jax.ShapeDtypeStruct((4, 2, ROWS, columns), BF)] * 2 + [jax.ShapeDtypeStruct((8, HD), F32)]
    return hidden_call(
        x_first_kernel, first, columns, scaled, weights, shapes, 10**8, "hidden_x_first", after
    )


def y_first(first, columns, scaled, weights, squares):
    gate, rows = columns + HD, 2 * ROWS
    parts = [gate + columns, gate, columns, columns, gate, gate, columns]
    shapes = [jax.ShapeDtypeStruct((rows, n), BF) for n in parts]
    return hidden_call(
        y_first_kernel, first, columns, scaled, weights, shapes, 10**9, "hidden_y_first", (squares,)
    )


def pass_on_kernel(up_add, up_pass, down_add, down_pass, below, above, _, to_above, to_below):
    gate = up_add.shape[1]
    to_above[:, :gate] = (up_add[...].astype(F32) + below[...].astype(F32)).astype(BF)
    to_above[:, gate:] = up_pass[...]
    to_below[:, :gate] = down_pass[...]
    to_below[:, gate:] = (down_add[...].astype(F32) + above[...].astype(F32)).astype(BF)


def pass_on(*sums):
    shape = jax.ShapeDtypeStruct((2 * ROWS, sums[0].shape[1] + sums[1].shape[1]), BF)
    return pl.pallas_call(
        pass_on_kernel,
        out_shape=[shape, shape],
        compiler_params=pltpu.CompilerParams(vmem_limit_bytes=VMEM),
        cost_estimate=pl.CostEstimate(flops=1000, bytes_accessed=1000, transcendentals=0),
        name="pass_on_sums",
    )(*sums)


def finish_kernel(here_ref, below_ref, above_ref, _, keep_ref, send_ref):
    sums = here_ref[...].astype(F32) + below_ref[...].astype(F32) + above_ref[...].astype(F32)
    keep_ref[...] = sums[:ROWS]
    send_ref[...] = sums[ROWS:].astype(BF)


def finish_y(here, below, above, after):
    shape = lambda t: jax.ShapeDtypeStruct((ROWS, here.shape[1]), t)
    return pl.pallas_call(
        finish_kernel,
        in_specs=[pl.BlockSpec()] * 4,
        out_shape=[shape(F32), shape(BF)],
        compiler_params=pltpu.CompilerParams(vmem_limit_bytes=VMEM),
        cost_estimate=pl.CostEstimate(flops=1000, bytes_accessed=1000, transcendentals=0),
        name="finish_y",
    )(here, below, above, after)


def add_kernel(keep_ref, got_ref, _, mine_ref, *send_refs):
    for k, ref in enumerate((mine_ref, *send_refs)):
        ref[...] = (keep_ref[k].astype(F32) + got_ref[k].astype(F32)).astype(ref.dtype)


def add_got(keep, got, after):
    held = pl.BlockSpec(memory_space=pl.ANY)
    return pl.pallas_call(
        add_kernel,
        in_specs=[pl.BlockSpec(), pl.BlockSpec(), held],
        out_shape=[jax.ShapeDtypeStruct(keep.shape[1:], t) for t in (F32, BF, BF, BF)],
        compiler_params=pltpu.CompilerParams(vmem_limit_bytes=VMEM),
        cost_estimate=pl.CostEstimate(flops=1000, bytes_accessed=1000, transcendentals=0),
        name="add_across_x",
    )(keep, got, after)


def activate(gate, up, rms):
    return (jax.nn.silu(gate / rms) * (up / rms)).astype(BF)


def finish_b_kernel(keep_ref, got_ref, out_ref, rms_ref):
    columns = out_ref.shape[1]
    sums = keep_ref[...] + got_ref[...].astype(F32)
    rms = jnp.sqrt(sums[:, columns : columns + HD] / D + 1e-05)
    rms_ref[...] = rms
    out_ref[...] = activate(sums[:, :columns], sums[:, columns + HD :], rms[:, :1])


def finish_b(keep, got):
    return pl.pallas_call(
        finish_b_kernel,
        out_shape=[jax.ShapeDtypeStruct((ROWS, B_COLS), BF), jax.ShapeDtypeStruct((ROWS, HD), F32)],
        compiler_params=pltpu.CompilerParams(vmem_limit_bytes=VMEM),
        cost_estimate=pl.CostEstimate(flops=10**6, bytes_accessed=1 << 20, transcendentals=10**5),
        name="finish_b",
    )(keep, got)


def finish_a_kernel(mine_ref, *refs):
    got, (b_ref, rms_ref, out_ref) = refs[:3], refs[3:]
    gate, up = (mine_ref[n] + sum(g[n].astype(F32) for g in got) for n in range(2))
    out_ref[:, :A_COLS] = activate(gate, up, rms_ref[:, :1])
    out_ref[:, A_COLS:] = b_ref[...]


def finish_a(mine, got, b_part, rms):
    return pl.pallas_call(
        finish_a_kernel,
        out_shape=jax.ShapeDtypeStruct((ROWS, HIDDEN), BF),
        compiler_params=pltpu.CompilerParams(vmem_limit_bytes=VMEM),
        cost_estimate=pl.CostEstimate(flops=10**6, bytes_accessed=1 << 20, transcendentals=10**5),
        name="finish_a",
    )(mine, *got, b_part, rms)


def y_sums(up_add, up_pass, down_add, down_pass, far_gate, far_up, token):
    from_below = over_batch(far_gate, 0, 1)
    from_above = over_batch(far_up, 0, -1)
    to_above, to_below = pass_on(up_add, up_pass, down_add, down_pass, from_below, from_above, token)
    return over_batch(to_above, 0, 1), over_batch(to_below, 0, -1)


def on_device(
    queries,
    new_key,
    new_value,
    prefix_keys,
    prefix_values,
    suffix_keys,
    suffix_values,
    suffix_lengths,
    out_weight,
    residual,
    norm_gain,
    gate_weight,
    up_weight,
):
    c = lax.axis_index("ctx")
    b = lax.axis_index("batch")
    xh, z = c // 4, c % 4
    xl, y, core = b // 8, b // 2 % 4, b % 2

    other_gate, other_up = over_batch(gate_weight, 0, 0, 1), over_batch(up_weight, 0, 0, 1)
    other_out = over_batch(out_weight, 0, 0, 1)
    own_gain = norm_gain.reshape(1, HALF)
    other_gain = over_batch(own_gain, 0, 0, 1)
    blocks = residual.reshape(4, 2, 2, ROWS, HALF)
    take = lambda k: lax.dynamic_slice(blocks, (z, 0, k, 0, 0), (1, 2, 1, ROWS, HALF)).reshape(96, HALF)
    residual_rows = jnp.concatenate([take(core), over_batch(take(1 - core), 0, 0, 1)], axis=1)

    def group_of(flip, s):
        return ((xh + flip) % 2 * 4 + (z - s) % 4).astype(jnp.int32).reshape(1)

    q_across = over_ctx(queries, 1, 0)
    own, token = own_prefix(group_of(0, 0), queries, prefix_keys, prefix_values)
    q2 = pair_up(queries, q_across, token)
    arrived = {0: None} | {s: over_ctx(q2, 0, s) for s in (1, 3, 2)}
    across = prefix_part(group_of(1, 0), q_across, None, prefix_keys, prefix_values, ())
    suffix_out, suffix_lse = suffix_part(queries, suffix_keys, suffix_values, new_key, new_value, suffix_lengths)
    parts, last = [own, over_ctx(across, 1, 0)], across
    for s in (1, 3, 2):
        for flip in (1, 0):
            after = (last,) if len(parts) < 5 else (last, parts[len(parts) - 4])
            group = group_of(flip, s)
            if len(parts) == 2:
                group, other_gate, other_up = lax.optimization_barrier((group, other_gate, other_up))
            last = prefix_part(group, arrived[s], flip, prefix_keys, prefix_values, after)
            parts.append(over_ctx(last, flip, -s))
    attended = merge_parts(parts, suffix_out, suffix_lse)
    everyone = lax.all_to_all(
        attended,
        "batch",
        0,
        0,
        axis_index_groups=SAME_CORE,
        tiled=True,
    ).reshape(384, 1024)
    gain, mine, *send = project(
        z.astype(jnp.int32).reshape(1), everyone, out_weight, other_out, own_gain, other_gain
    )
    for s in (1, 3, 2):
        mine = mine + over_ctx(send[s - 1], 0, s).astype(F32)
    mine = mine.astype(BF)
    across = over_ctx(mine, 1, 0)
    mixed = mine.astype(F32) + across.astype(F32)
    chunk = (residual_rows.astype(F32) + mixed).astype(BF)
    pieces = [chunk] + [over_ctx(chunk, 0, s) for s in (1, 3, 2)]
    piece_z = [z, (z - 1) % 4, (z - 3) % 4, (z - 2) % 4]

    blocks = [2 * pz + e for pz in piece_z for e in range(2)]
    place = [(block // 4 - xl) % 2 * 4 + (block % 4 - y) % 4 for block in blocks] + blocks + [core]
    place = jnp.stack(place).astype(jnp.int32)
    scaled, squares, their_columns = fill(place, pieces, gain)
    weights = hold(chunk, gate_weight, other_gate, up_weight, other_up)
    b_first = y_first(A_COLS, B_COLS, scaled, weights, squares)
    a_first = x_first(0, A_COLS, scaled, weights, b_first[-1])
    received = y_sums(*b_first[1:], a_first[2])
    stream, token = assemble(place, pieces, over_batch(their_columns, 0, 0, 1))
    b_keep, b_send = finish_y(b_first[0], *received, token)
    b_part, rms = finish_b(b_keep, over_batch(b_send, 1, 0))
    mine, *sends = add_got(a_first[0], over_batch(a_first[1], 1, 0), b_send)
    activation = finish_a(mine, [over_batch(sends[s - 1], 0, s) for s in (2, 1, 3)], b_part, rms)
    return (stream, activation)


def solution(mesh):
    in_specs = (
        P("batch", "ctx"),
        P("batch", "ctx"),
        P("batch", "ctx"),
        P("ctx", None),
        P("ctx", None),
        P("batch", None, "ctx"),
        P("batch", None, "ctx"),
        P("batch"),
        P("ctx", "batch"),
        P(None, "batch"),
        P("batch"),
        P("batch", "ctx"),
        P("batch", "ctx"),
    )
    out_specs = (P(None, "batch"), P("batch", "ctx"))
    return jax.shard_map(
        on_device, mesh=mesh, in_specs=in_specs, out_specs=out_specs, check_vma=False
    )
```

```python
import functools

import jax
import jax.numpy as jnp
from jax import lax
from jax.experimental import pallas as pl
from jax.experimental.pallas import tpu as pltpu
from jax.sharding import PartitionSpec as P

D = 8192
KV = 8
HD = 128
SUF = 128
GROUP = 8
ROWS = 48
QROWS = ROWS * GROUP
META = 16
PAYLOAD = QROWS + QROWS // 128 * META
PRE = 2048
HALF = 512
HIDDEN = 3584
A_COLS = 1536
B_COLS = HIDDEN - A_COLS
TILE = 512
SAME_CORE = [list(range(0, 16, 2)), list(range(1, 16, 2))]
BF = jnp.bfloat16
F32 = jnp.float32
VMEM = 16 << 20
Q_TILE = 192
OWN_COPIES = 4
LOG2E = 1.4426950408889634


def ctx_perm(flip, s):
    return [(x * 4 + z, (x ^ flip) * 4 + (z + s) % 4) for x in range(2) for z in range(4)]


def batch_perm(flip_x, s, flip_core):
    return [
        (x * 8 + y * 2 + k, (x ^ flip_x) * 8 + (y + s) % 4 * 2 + (k ^ flip_core))
        for x in range(2)
        for y in range(4)
        for k in range(2)
    ]


def over_ctx(v, flip, s):
    return lax.ppermute(v, "ctx", ctx_perm(flip, s))


def over_batch(v, flip_x, s, flip_core=0):
    return lax.ppermute(v, "batch", batch_perm(flip_x, s, flip_core))


def nt_dot(a, b):
    return lax.dot_general(a, b, (((1,), (1,)), ((), ())), preferred_element_type=F32)


def heads_as_rows(q):
    return jnp.concatenate([q[:, h * HD : (h + 1) * HD] for h in range(GROUP)], axis=0)


def split3(v):
    hi = v.astype(BF).astype(F32)
    rest = v - hi
    mid = rest.astype(BF).astype(F32)
    return hi, mid, rest - mid


def attend_prefix(q, k, v):
    scale = 1.0 / (HD**0.5)
    outs, sums = [], []
    for t in range(QROWS // Q_TILE):
        s = nt_dot(q[t * Q_TILE : (t + 1) * Q_TILE], k)
        top = jnp.max(s, axis=1, keepdims=True)
        w = jnp.exp2((s - top) * (scale * LOG2E))
        total = jnp.sum(w, axis=1, keepdims=True)
        o = jnp.dot(w.astype(BF), v, preferred_element_type=F32)
        outs.append((o / total).astype(BF))
        sums.append(top * scale + jnp.log(total))
    return outs, jnp.concatenate(sums, axis=0)


def put_payload(put, outs, lse):
    column = lax.broadcasted_iota(jnp.int32, (128, 128), 1)
    for t, o in enumerate(outs):
        put(t * Q_TILE, o)
    for t in range(QROWS // 128):
        hi, mid, lo = split3(lse[t * 128 : (t + 1) * 128])
        parts = jnp.where(column == 0, hi, jnp.where(column == 1, mid, jnp.where(column == 2, lo, 0.0)))
        put(QROWS + t * META, parts.T[:META].astype(BF))


def prefix_kernel(which, group_ref, q_ref, k_ref, v_ref, *refs):
    out_ref = refs[-1]
    at = pl.ds(pl.multiple_of(group_ref[0] * HD, HD), HD)
    q = heads_as_rows(q_ref[...] if which is None else q_ref[which])

    def put(row, value):
        out_ref[row : row + value.shape[0], :] = value

    put_payload(put, *attend_prefix(q, k_ref[:, at], v_ref[:, at]))


def own_prefix_kernel(group_ref, q_ref, k_ref, v_ref, out_ref, token_ref, k_held, v_held, sems):
    token_ref[...] = jnp.zeros_like(token_ref)
    at = pl.ds(pl.multiple_of(group_ref[0] * HD, HD), HD)
    copies = []
    for n, (source, held) in enumerate(((k_ref, k_held), (v_ref, v_held))):
        for m in range(OWN_COPIES):
            rows = pl.ds(m * (PRE // OWN_COPIES), PRE // OWN_COPIES)
            copies.append(pltpu.make_async_copy(source.at[rows, at], held.at[rows], sems.at[n, m]))
    for copy in copies:
        copy.start()
    for copy in copies:
        copy.wait()

    def put(row, value):
        out_ref[row : row + value.shape[0], :] = value

    put_payload(put, *attend_prefix(heads_as_rows(q_ref[...]), k_held[...], v_held[...]))


def own_prefix(group, q, keys, values):
    held = pl.BlockSpec(memory_space=pl.ANY)
    return pl.pallas_call(
        own_prefix_kernel,
        in_specs=[pl.BlockSpec(memory_space=pltpu.SMEM), pl.BlockSpec(), held, held],
        out_shape=[jax.ShapeDtypeStruct((PAYLOAD, HD), BF), jax.ShapeDtypeStruct((8, HD), F32)],
        scratch_shapes=[pltpu.VMEM((PRE, HD), BF), pltpu.VMEM((PRE, HD), BF), pltpu.SemaphoreType.DMA((2, OWN_COPIES))],
        compiler_params=pltpu.CompilerParams(vmem_limit_bytes=59 << 20),
        cost_estimate=pl.CostEstimate(
            flops=4 * QROWS * PRE * HD, bytes_accessed=2 * 2 * PRE * HD, transcendentals=QROWS * PRE
        ),
        name="own_prefix",
    )(group, q, keys, values)


def prefix_part(group, q, which, keys, values, after):
    vmem = pl.BlockSpec(memory_space=pltpu.VMEM)
    return pl.pallas_call(
        functools.partial(prefix_kernel, which),
        in_specs=[pl.BlockSpec(memory_space=pltpu.SMEM), pl.BlockSpec(), vmem, vmem]
        + [pl.BlockSpec(memory_space=pl.ANY)] * len(after),
        out_shape=jax.ShapeDtypeStruct((PAYLOAD, HD), BF),
        compiler_params=pltpu.CompilerParams(vmem_limit_bytes=VMEM),
        cost_estimate=pl.CostEstimate(
            flops=4 * QROWS * PRE * HD, bytes_accessed=2 * 2 * PRE * HD, transcendentals=QROWS * PRE
        ),
        name="prefix_part",
    )(group, q, keys, values, *after)


def pair_kernel(mine_ref, across_ref, _, out_ref):
    out_ref[0] = mine_ref[...]
    out_ref[1] = across_ref[...]


def pair_up(mine, across, after):
    return pl.pallas_call(
        pair_kernel,
        out_shape=jax.ShapeDtypeStruct((2, *mine.shape), mine.dtype),
        compiler_params=pltpu.CompilerParams(vmem_limit_bytes=VMEM),
        cost_estimate=pl.CostEstimate(flops=0, bytes_accessed=4 * mine.size * 2, transcendentals=0),
        name="pair_up",
    )(mine, across, after)


SUF_LEAVES = 16


def suffix_kernel(q_ref, k_ref, v_ref, nk_ref, nv_ref, len_ref, o_ref, lse_ref):
    scale = 1.0 / (HD**0.5)
    n = SUF_LEAVES * GROUP
    q = heads_as_rows(q_ref[...])
    s = nt_dot(q, k_ref[...]) * scale
    lengths = jnp.concatenate([len_ref[...][:, :1]] * GROUP, axis=0)
    row = lax.broadcasted_iota(jnp.int32, (n, 1), 0) % SUF_LEAVES
    slot = lax.broadcasted_iota(jnp.int32, s.shape, 1) - row * SUF
    s = jnp.where((slot >= 0) & (slot < lengths), s, -1e30)
    fresh_key = jnp.concatenate([nk_ref[...].astype(F32)] * GROUP, axis=0)
    fresh = jnp.sum(q.astype(F32) * fresh_key, axis=1, keepdims=True) * scale
    top = jnp.maximum(jnp.max(s, axis=1, keepdims=True), fresh)
    w = jnp.exp(s - top)
    wn = jnp.exp(fresh - top)
    total = jnp.sum(w, axis=1, keepdims=True) + wn
    o = jnp.dot(w.astype(BF), v_ref[...], preferred_element_type=F32)
    fresh_value = jnp.concatenate([nv_ref[...].astype(F32)] * GROUP, axis=0)
    o = (o + wn.astype(BF).astype(F32) * fresh_value) / total
    lse = jnp.broadcast_to(top + jnp.log(total), o.shape)
    for h in range(GROUP):
        o_ref[h] = o[h * SUF_LEAVES : (h + 1) * SUF_LEAVES]
        lse_ref[h] = lse[h * SUF_LEAVES : (h + 1) * SUF_LEAVES]


def suffix_part(q, keys, values, new_key, new_value, lengths):
    shape = jax.ShapeDtypeStruct((GROUP, ROWS, HD), F32)
    leaf = lambda w: pl.BlockSpec((SUF_LEAVES, w), lambda i: (i, 0))
    cached = pl.BlockSpec((SUF_LEAVES * SUF, HD), lambda i: (i, 0))
    return pl.pallas_call(
        suffix_kernel,
        grid=(ROWS // SUF_LEAVES,),
        in_specs=[leaf(GROUP * HD), cached, cached, leaf(HD), leaf(HD), leaf(HD)],
        out_specs=[pl.BlockSpec((GROUP, SUF_LEAVES, HD), lambda i: (0, i, 0))] * 2,
        out_shape=[shape, shape],
        compiler_params=pltpu.CompilerParams(vmem_limit_bytes=VMEM),
        cost_estimate=pl.CostEstimate(flops=4 * QROWS * 2048 * HD, bytes_accessed=4 << 20, transcendentals=QROWS * 2048),
        name="suffix_part",
    )(
        q,
        keys.reshape(ROWS * SUF, HD),
        values.reshape(ROWS * SUF, HD),
        new_key,
        new_value,
        jnp.broadcast_to(lengths[:, None], (ROWS, HD)),
    )


def merge_kernel(*refs):
    parts, (so_ref, sl_ref, out_ref, held) = refs[:KV], refs[KV:]

    def rows_of(at, n):
        return [p[at : at + n, :].astype(F32) for p in parts]

    for t in range(QROWS // 128):
        rows = [m[0:1] + m[1:2] + m[2:3] for m in rows_of(QROWS + t * META, META)]
        lse = jnp.concatenate(rows, axis=0).T
        suf_lse = sl_ref[t * 128 : (t + 1) * 128, :1]
        top = jnp.maximum(jnp.max(lse, axis=1, keepdims=True), suf_lse)
        w = jnp.exp(lse - top)
        ws = jnp.exp(suf_lse - top)
        total = jnp.sum(w, axis=1, keepdims=True) + ws
        o = so_ref[t * 128 : (t + 1) * 128, :] * ws
        for i, p in enumerate(rows_of(t * 128, 128)):
            o = o + p * w[:, i : i + 1]
        held[t * 128 : (t + 1) * 128, :] = (o / total).astype(BF)
    for n in range(8):
        for h in range(GROUP):
            out_ref[n, :, h * HD : (h + 1) * HD] = held[h * ROWS : (h + 1) * ROWS, :]


def merge_parts(parts, suffix_out, suffix_lse):
    return pl.pallas_call(
        merge_kernel,
        out_shape=jax.ShapeDtypeStruct((8, ROWS, GROUP * HD), BF),
        scratch_shapes=[pltpu.VMEM((QROWS, HD), BF)],
        compiler_params=pltpu.CompilerParams(vmem_limit_bytes=VMEM),
        cost_estimate=pl.CostEstimate(flops=QROWS * HD * 20, bytes_accessed=2 << 20, transcendentals=QROWS * 10),
        name="merge_parts",
    )(*parts, suffix_out.reshape(QROWS, HD), suffix_lse.reshape(QROWS, HD))


def project_kernel(z_ref, a_ref, own_w_ref, other_w_ref, g0_ref, g1_ref, gain_ref, mine_ref, *send_refs):
    gain_ref[:, :HALF] = g0_ref[...].astype(F32)
    gain_ref[:, HALF:] = g1_ref[...].astype(F32)
    z = z_ref[0]
    pieces = [a_ref[pl.ds(pl.multiple_of((z + s) % 4 * 96, 16), 96), :] for s in range(4)]
    a = jnp.concatenate(pieces, axis=0)
    for half, w_ref in enumerate((own_w_ref, other_w_ref)):
        y = jnp.dot(a, w_ref[...], preferred_element_type=F32)
        at = slice(half * HALF, (half + 1) * HALF)
        mine_ref[:, at] = y[:96]
        for s, ref in enumerate(send_refs):
            ref[:, at] = y[(s + 1) * 96 : (s + 2) * 96].astype(BF)


def project(z, attended, own_w, other_w, own_gain, other_gain):
    vmem = pl.BlockSpec(memory_space=pltpu.VMEM)
    return pl.pallas_call(
        project_kernel,
        in_specs=[pl.BlockSpec(memory_space=pltpu.SMEM)] + [vmem] * 5,
        out_specs=[vmem] * 5,
        out_shape=[jax.ShapeDtypeStruct((1, 2 * HALF), F32), jax.ShapeDtypeStruct((96, 2 * HALF), F32)] + [jax.ShapeDtypeStruct((96, 2 * HALF), BF)] * 3,
        compiler_params=pltpu.CompilerParams(vmem_limit_bytes=VMEM),
        cost_estimate=pl.CostEstimate(flops=2 * 384 * 1024 * 1024, bytes_accessed=4 << 20, transcendentals=0),
        name="project",
    )(z, attended, own_w, other_w, own_gain, other_gain)


def fill_kernel(place_ref, *refs):
    pieces, (gain_ref, scaled_ref, squares_ref, theirs_ref) = refs[:4], refs[4:]
    for j, piece in enumerate(pieces):
        for e in range(2):
            sent = pl.multiple_of(place_ref[j * 2 + e] * ROWS, 16)
            block = pl.multiple_of(place_ref[8 + j * 2 + e] * ROWS, 16)
            rows = piece[e * ROWS : (e + 1) * ROWS, :]
            wide = rows.astype(F32)
            scaled_ref[pl.ds(sent, ROWS), :] = (wide * gain_ref[...]).astype(BF)
            theirs_ref[pl.ds(block, ROWS), :] = rows[:, HALF:]
            squares = jnp.sum(wide * wide, axis=1, keepdims=True)
            squares_ref[pl.ds(sent, ROWS), :] = jnp.broadcast_to(squares, (ROWS, HD))


def fill(place, pieces, gain):
    vmem = pl.BlockSpec(memory_space=pltpu.VMEM)
    return pl.pallas_call(
        fill_kernel,
        in_specs=[pl.BlockSpec(memory_space=pltpu.SMEM)] + [vmem] * 5,
        out_shape=[
            jax.ShapeDtypeStruct((384, 2 * HALF), BF),
            jax.ShapeDtypeStruct((384, HD), F32),
            jax.ShapeDtypeStruct((384, HALF), BF),
        ],
        compiler_params=pltpu.CompilerParams(vmem_limit_bytes=VMEM),
        cost_estimate=pl.CostEstimate(flops=384 * 4096, bytes_accessed=2 << 20, transcendentals=0),
        name="scale_rows",
    )(place, *pieces, gain)


def assemble_kernel(place_ref, *refs):
    pieces, (theirs_ref, out_ref, token_ref) = refs[:4], refs[4:]
    token_ref[...] = jnp.zeros_like(token_ref)
    core = place_ref[16]
    for j, piece in enumerate(pieces):
        for e in range(2):
            block = place_ref[8 + j * 2 + e]
            ours = pl.multiple_of((block * 2 + core) * ROWS, 16)
            other = pl.multiple_of((block * 2 + 1 - core) * ROWS, 16)
            out_ref[pl.ds(ours, ROWS), :] = piece[e * ROWS : (e + 1) * ROWS, :HALF]
            out_ref[pl.ds(other, ROWS), :] = theirs_ref[pl.ds(pl.multiple_of(block * ROWS, 16), ROWS), :]


def assemble(place, pieces, theirs):
    return pl.pallas_call(
        assemble_kernel,
        in_specs=[pl.BlockSpec(memory_space=pltpu.SMEM)] + [pl.BlockSpec()] * 5,
        out_shape=[jax.ShapeDtypeStruct((768, HALF), BF), jax.ShapeDtypeStruct((8, HD), F32)],
        compiler_params=pltpu.CompilerParams(vmem_limit_bytes=VMEM),
        cost_estimate=pl.CostEstimate(flops=1000, bytes_accessed=1000, transcendentals=0),
        name="assemble_stream",
    )(place, *pieces, theirs)


def hold_kernel(_, *refs):
    sources, places, sems = refs[:4], refs[4:8], refs[8]
    copies = [pltpu.make_async_copy(a, b, sems.at[i]) for i, (a, b) in enumerate(zip(sources, places))]
    for copy in copies:
        copy.start()
    for copy in copies:
        copy.wait()


def hold(after, *arrays):
    return pl.pallas_call(
        hold_kernel,
        in_specs=[pl.BlockSpec()] + [pl.BlockSpec(memory_space=pl.ANY)] * 4,
        out_specs=[pl.BlockSpec(memory_space=pltpu.VMEM)] * 4,
        out_shape=[jax.ShapeDtypeStruct(a.shape, a.dtype) for a in arrays],
        scratch_shapes=[pltpu.SemaphoreType.DMA((4,))],
        compiler_params=pltpu.CompilerParams(vmem_limit_bytes=24 << 20),
        cost_estimate=pl.CostEstimate(flops=0, bytes_accessed=sum(a.size * 4 for a in arrays), transcendentals=0),
        name="hold_weights",
    )(after, *arrays)


def weight_tiles(first, columns, weights):
    ends = range(columns % TILE or TILE, columns + 1, TILE)
    for end in ends:
        at = slice(max(end - TILE, 0), end)
        yield at, [w[:, first + at.start : first + at.stop] for w in weights]


def hidden_sums(s, own_gate, other_gate, own_up, other_up):
    out = []
    for own, other in ((own_gate, other_gate), (own_up, other_up)):
        y = jnp.dot(s[:, :HALF], own, preferred_element_type=F32)
        out.append(y + jnp.dot(s[:, HALF:], other, preferred_element_type=F32))
    return out


def x_first_kernel(first, columns, s_ref, g0, g1, u0, u1, *refs):
    keep_ref, send_ref, token_ref = refs[-3:]
    token_ref[...] = jnp.zeros_like(token_ref)
    for to, blocks in weight_tiles(first, columns, (g0, g1, u0, u1)):
        for n, y in enumerate(hidden_sums(s_ref[...], *blocks)):
            for k in range(4):
                keep_ref[k, n, :, to] = y[k * ROWS : (k + 1) * ROWS].astype(BF)
                send_ref[k, n, :, to] = y[(4 + k) * ROWS : (5 + k) * ROWS].astype(BF)


def y_first_kernel(first, columns, s_ref, g0, g1, u0, u1, squares_ref, *refs):
    here_ref, up_add, up_pass, down_add, down_pass, far_gate, far_up = refs
    up, down, far = (up_add, up_pass), (down_pass, down_add), (far_gate, far_up)

    def put(n, to, y):
        for x in range(2):
            at = slice(x * ROWS, (x + 1) * ROWS)
            part = [y[(x * 4 + k) * ROWS : (x * 4 + k + 1) * ROWS] for k in range(4)]
            here_ref[at, to.start + n * (columns + HD) : to.stop + n * (columns + HD)] = part[0].astype(BF)
            for ref, value in ((up[n], part[1]), (far[n], part[2]), (down[n], part[3])):
                ref[at, to] = value.astype(BF)

    put(0, slice(columns, columns + HD), squares_ref[...])
    for to, blocks in weight_tiles(first, columns, (g0, g1, u0, u1)):
        for n, y in enumerate(hidden_sums(s_ref[...], *blocks)):
            put(n, to, y)


def hidden_call(kernel, first, columns, scaled, weights, shapes, flops, name, more):
    return pl.pallas_call(
        functools.partial(kernel, first, columns),
        in_specs=[pl.BlockSpec()] + [pl.BlockSpec(memory_space=pltpu.VMEM)] * 4 + [pl.BlockSpec()] * len(more),
        out_shape=shapes,
        compiler_params=pltpu.CompilerParams(vmem_limit_bytes=12 << 20),
        cost_estimate=pl.CostEstimate(flops=flops, bytes_accessed=flops // 1000, transcendentals=0),
        name=name,
    )(scaled, *weights, *more)


def x_first(first, columns, scaled, weights, *after):
    shapes = [jax.ShapeDtypeStruct((4, 2, ROWS, columns), BF)] * 2 + [jax.ShapeDtypeStruct((8, HD), F32)]
    return hidden_call(
        x_first_kernel, first, columns, scaled, weights, shapes, 10**8, "hidden_x_first", after
    )


def y_first(first, columns, scaled, weights, squares):
    gate, rows = columns + HD, 2 * ROWS
    parts = [gate + columns, gate, columns, columns, gate, gate, columns]
    shapes = [jax.ShapeDtypeStruct((rows, n), BF) for n in parts]
    return hidden_call(
        y_first_kernel, first, columns, scaled, weights, shapes, 10**9, "hidden_y_first", (squares,)
    )


def pass_on_kernel(up_add, down_add, below, above, _, to_above, to_below):
    to_above[...] = (up_add[...].astype(F32) + below[...].astype(F32)).astype(BF)
    to_below[...] = (down_add[...].astype(F32) + above[...].astype(F32)).astype(BF)


def pass_on(*sums):
    shapes = [jax.ShapeDtypeStruct(v.shape, BF) for v in sums[:2]]
    return pl.pallas_call(
        pass_on_kernel,
        out_shape=shapes,
        compiler_params=pltpu.CompilerParams(vmem_limit_bytes=VMEM),
        cost_estimate=pl.CostEstimate(flops=1000, bytes_accessed=1000, transcendentals=0),
        name="pass_on_sums",
    )(*sums)


def finish_kernel(here_ref, below_gate, below_up, above_gate, above_up, _, keep_ref, send_ref):
    gate = below_gate.shape[1]
    for at, below, above in ((slice(0, gate), below_gate, above_gate), (slice(gate, None), below_up, above_up)):
        sums = here_ref[:, at].astype(F32) + below[...].astype(F32) + above[...].astype(F32)
        keep_ref[:, at] = sums[:ROWS]
        send_ref[:, at] = sums[ROWS:].astype(BF)


def finish_y(here, received, after):
    shape = lambda t: jax.ShapeDtypeStruct((ROWS, here.shape[1]), t)
    return pl.pallas_call(
        finish_kernel,
        out_shape=[shape(F32), shape(BF)],
        compiler_params=pltpu.CompilerParams(vmem_limit_bytes=VMEM),
        cost_estimate=pl.CostEstimate(flops=1000, bytes_accessed=1000, transcendentals=0),
        name="finish_y",
    )(here, *received, after)


def add_kernel(keep_ref, got_ref, _, mine_ref, *send_refs):
    for k, ref in enumerate((mine_ref, *send_refs)):
        ref[...] = (keep_ref[k].astype(F32) + got_ref[k].astype(F32)).astype(ref.dtype)


def add_got(keep, got, after):
    held = pl.BlockSpec(memory_space=pl.ANY)
    return pl.pallas_call(
        add_kernel,
        in_specs=[pl.BlockSpec(), pl.BlockSpec(), held],
        out_shape=[jax.ShapeDtypeStruct(keep.shape[1:], t) for t in (F32, BF, BF, BF)],
        compiler_params=pltpu.CompilerParams(vmem_limit_bytes=VMEM),
        cost_estimate=pl.CostEstimate(flops=1000, bytes_accessed=1000, transcendentals=0),
        name="add_across_x",
    )(keep, got, after)


def activate(gate, up, rms):
    return (jax.nn.silu(gate / rms) * (up / rms)).astype(BF)


def finish_b_kernel(keep_ref, got_ref, out_ref, rms_ref):
    columns = out_ref.shape[1]
    sums = keep_ref[...] + got_ref[...].astype(F32)
    rms = jnp.sqrt(sums[:, columns : columns + HD] / D + 1e-05)
    rms_ref[...] = rms
    out_ref[...] = activate(sums[:, :columns], sums[:, columns + HD :], rms[:, :1])


def finish_b(keep, got):
    return pl.pallas_call(
        finish_b_kernel,
        out_shape=[jax.ShapeDtypeStruct((ROWS, B_COLS), BF), jax.ShapeDtypeStruct((ROWS, HD), F32)],
        compiler_params=pltpu.CompilerParams(vmem_limit_bytes=VMEM),
        cost_estimate=pl.CostEstimate(flops=10**6, bytes_accessed=1 << 20, transcendentals=10**5),
        name="finish_b",
    )(keep, got)


def finish_a_kernel(mine_ref, *refs):
    got, (b_ref, rms_ref, out_ref) = refs[:3], refs[3:]
    gate, up = (mine_ref[n] + sum(g[n].astype(F32) for g in got) for n in range(2))
    out_ref[:, :A_COLS] = activate(gate, up, rms_ref[:, :1])
    out_ref[:, A_COLS:] = b_ref[...]


def finish_a(mine, got, b_part, rms):
    return pl.pallas_call(
        finish_a_kernel,
        out_shape=jax.ShapeDtypeStruct((ROWS, HIDDEN), BF),
        compiler_params=pltpu.CompilerParams(vmem_limit_bytes=VMEM),
        cost_estimate=pl.CostEstimate(flops=10**6, bytes_accessed=1 << 20, transcendentals=10**5),
        name="finish_a",
    )(mine, *got, b_part, rms)


def y_sums(up_add, up_pass, down_add, down_pass, far_gate, far_up, token):
    from_below = over_batch(far_gate, 0, 1)
    from_above = over_batch(far_up, 0, -1)
    gate_above, up_below = pass_on(up_add, down_add, from_below, from_above, token)
    above = over_batch(gate_above, 0, 1), over_batch(up_pass, 0, 1)
    below = over_batch(down_pass, 0, -1), over_batch(up_below, 0, -1)
    return (*above, *below)


def on_device(
    queries,
    new_key,
    new_value,
    prefix_keys,
    prefix_values,
    suffix_keys,
    suffix_values,
    suffix_lengths,
    out_weight,
    residual,
    norm_gain,
    gate_weight,
    up_weight,
):
    c = lax.axis_index("ctx")
    b = lax.axis_index("batch")
    xh, z = c // 4, c % 4
    xl, y, core = b // 8, b // 2 % 4, b % 2

    other_gate, other_up = over_batch(gate_weight, 0, 0, 1), over_batch(up_weight, 0, 0, 1)
    other_out = over_batch(out_weight, 0, 0, 1)
    own_gain = norm_gain.reshape(1, HALF)
    other_gain = over_batch(own_gain, 0, 0, 1)
    blocks = residual.reshape(4, 2, 2, ROWS, HALF)
    take = lambda k: lax.dynamic_slice(blocks, (z, 0, k, 0, 0), (1, 2, 1, ROWS, HALF)).reshape(96, HALF)
    residual_rows = jnp.concatenate([take(core), over_batch(take(1 - core), 0, 0, 1)], axis=1)

    def group_of(flip, s):
        return ((xh + flip) % 2 * 4 + (z - s) % 4).astype(jnp.int32).reshape(1)

    q_across = over_ctx(queries, 1, 0)
    own, token = own_prefix(group_of(0, 0), queries, prefix_keys, prefix_values)
    q2 = pair_up(queries, q_across, token)
    arrived = {0: None} | {s: over_ctx(q2, 0, s) for s in (1, 3, 2)}
    across = prefix_part(group_of(1, 0), q_across, None, prefix_keys, prefix_values, ())
    suffix_out, suffix_lse = suffix_part(queries, suffix_keys, suffix_values, new_key, new_value, suffix_lengths)
    parts, last = [own, over_ctx(across, 1, 0)], across
    for s in (1, 3, 2):
        for flip in (1, 0):
            after = (last,) if len(parts) < 5 else (last, parts[len(parts) - 4])
            group = group_of(flip, s)
            if len(parts) == 2:
                group, other_gate, other_up = lax.optimization_barrier((group, other_gate, other_up))
            last = prefix_part(group, arrived[s], flip, prefix_keys, prefix_values, after)
            parts.append(over_ctx(last, flip, -s))
    attended = merge_parts(parts, suffix_out, suffix_lse)
    everyone = lax.all_to_all(
        attended,
        "batch",
        0,
        0,
        axis_index_groups=SAME_CORE,
        tiled=True,
    ).reshape(384, 1024)
    gain, mine, *send = project(
        z.astype(jnp.int32).reshape(1), everyone, out_weight, other_out, own_gain, other_gain
    )
    for s in (1, 3, 2):
        mine = mine + over_ctx(send[s - 1], 0, s).astype(F32)
    mine = mine.astype(BF)
    across = over_ctx(mine, 1, 0)
    mixed = mine.astype(F32) + across.astype(F32)
    chunk = (residual_rows.astype(F32) + mixed).astype(BF)
    pieces = [chunk] + [over_ctx(chunk, 0, s) for s in (1, 3, 2)]
    piece_z = [z, (z - 1) % 4, (z - 3) % 4, (z - 2) % 4]

    blocks = [2 * pz + e for pz in piece_z for e in range(2)]
    place = [(block // 4 - xl) % 2 * 4 + (block % 4 - y) % 4 for block in blocks] + blocks + [core]
    place = jnp.stack(place).astype(jnp.int32)
    scaled, squares, their_columns = fill(place, pieces, gain)
    weights = hold(chunk, gate_weight, other_gate, up_weight, other_up)
    b_first = y_first(A_COLS, B_COLS, scaled, weights, squares)
    a_first = x_first(0, A_COLS, scaled, weights, b_first[-1])
    received = y_sums(*b_first[1:], a_first[2])
    stream, token = assemble(place, pieces, over_batch(their_columns, 0, 0, 1))
    b_keep, b_send = finish_y(b_first[0], received, token)
    b_part, rms = finish_b(b_keep, over_batch(b_send, 1, 0))
    mine, *sends = add_got(a_first[0], over_batch(a_first[1], 1, 0), b_send)
    activation = finish_a(mine, [over_batch(sends[s - 1], 0, s) for s in (2, 1, 3)], b_part, rms)
    return (stream, activation)


def solution(mesh):
    in_specs = (
        P("batch", "ctx"),
        P("batch", "ctx"),
        P("batch", "ctx"),
        P("ctx", None),
        P("ctx", None),
        P("batch", None, "ctx"),
        P("batch", None, "ctx"),
        P("batch"),
        P("ctx", "batch"),
        P(None, "batch"),
        P("batch"),
        P("batch", "ctx"),
        P("batch", "ctx"),
    )
    out_specs = (P(None, "batch"), P("batch", "ctx"))
    return jax.shard_map(
        on_device, mesh=mesh, in_specs=in_specs, out_specs=out_specs, check_vma=False
    )
```

```python
import functools

import jax
import jax.numpy as jnp
from jax import lax
from jax.experimental import pallas as pl
from jax.experimental.pallas import tpu as pltpu
from jax.sharding import PartitionSpec as P

D = 8192
KV = 8
HD = 128
SUF = 128
GROUP = 8
ROWS = 48
QROWS = ROWS * GROUP
META = 16
PAYLOAD = QROWS + QROWS // 128 * META
PRE = 2048
HALF = 512
HIDDEN = 3584
A_COLS = 1536
B_COLS = HIDDEN - A_COLS
TILE = 512
SAME_CORE = [list(range(0, 16, 2)), list(range(1, 16, 2))]
BF = jnp.bfloat16
F32 = jnp.float32
VMEM = 16 << 20
Q_TILE = 192
OWN_COPIES = 4
LOG2E = 1.4426950408889634


def ctx_perm(flip, s):
    return [(x * 4 + z, (x ^ flip) * 4 + (z + s) % 4) for x in range(2) for z in range(4)]


def batch_perm(flip_x, s, flip_core):
    return [
        (x * 8 + y * 2 + k, (x ^ flip_x) * 8 + (y + s) % 4 * 2 + (k ^ flip_core))
        for x in range(2)
        for y in range(4)
        for k in range(2)
    ]


def over_ctx(v, flip, s):
    return lax.ppermute(v, "ctx", ctx_perm(flip, s))


def over_batch(v, flip_x, s, flip_core=0):
    return lax.ppermute(v, "batch", batch_perm(flip_x, s, flip_core))


def nt_dot(a, b):
    return lax.dot_general(a, b, (((1,), (1,)), ((), ())), preferred_element_type=F32)


def heads_as_rows(q):
    return jnp.concatenate([q[:, h * HD : (h + 1) * HD] for h in range(GROUP)], axis=0)


def split3(v):
    hi = v.astype(BF).astype(F32)
    rest = v - hi
    mid = rest.astype(BF).astype(F32)
    return hi, mid, rest - mid


def attend_prefix(q, k, v):
    scale = 1.0 / (HD**0.5)
    outs, sums = [], []
    for t in range(QROWS // Q_TILE):
        s = nt_dot(q[t * Q_TILE : (t + 1) * Q_TILE], k)
        top = jnp.max(s, axis=1, keepdims=True)
        w = jnp.exp2((s - top) * (scale * LOG2E))
        total = jnp.sum(w, axis=1, keepdims=True)
        o = jnp.dot(w.astype(BF), v, preferred_element_type=F32)
        outs.append((o / total).astype(BF))
        sums.append(top * scale + jnp.log(total))
    return outs, jnp.concatenate(sums, axis=0)


def put_payload(put, outs, lse):
    column = lax.broadcasted_iota(jnp.int32, (128, 128), 1)
    for t, o in enumerate(outs):
        put(t * Q_TILE, o)
    for t in range(QROWS // 128):
        hi, mid, lo = split3(lse[t * 128 : (t + 1) * 128])
        parts = jnp.where(column == 0, hi, jnp.where(column == 1, mid, jnp.where(column == 2, lo, 0.0)))
        put(QROWS + t * META, parts.T[:META].astype(BF))


def prefix_kernel(which, group_ref, q_ref, k_ref, v_ref, *refs):
    out_ref = refs[-1]
    at = pl.ds(pl.multiple_of(group_ref[0] * HD, HD), HD)
    q = heads_as_rows(q_ref[...] if which is None else q_ref[which])

    def put(row, value):
        out_ref[row : row + value.shape[0], :] = value

    put_payload(put, *attend_prefix(q, k_ref[:, at], v_ref[:, at]))


def own_prefix_kernel(group_ref, q_ref, k_ref, v_ref, out_ref, token_ref, k_held, v_held, sems):
    token_ref[...] = jnp.zeros_like(token_ref)
    at = pl.ds(pl.multiple_of(group_ref[0] * HD, HD), HD)
    copies = []
    for n, (source, held) in enumerate(((k_ref, k_held), (v_ref, v_held))):
        for m in range(OWN_COPIES):
            rows = pl.ds(m * (PRE // OWN_COPIES), PRE // OWN_COPIES)
            copies.append(pltpu.make_async_copy(source.at[rows, at], held.at[rows], sems.at[n, m]))
    for copy in copies:
        copy.start()
    for copy in copies:
        copy.wait()

    def put(row, value):
        out_ref[row : row + value.shape[0], :] = value

    put_payload(put, *attend_prefix(heads_as_rows(q_ref[...]), k_held[...], v_held[...]))


def own_prefix(group, q, keys, values):
    held = pl.BlockSpec(memory_space=pl.ANY)
    return pl.pallas_call(
        own_prefix_kernel,
        in_specs=[pl.BlockSpec(memory_space=pltpu.SMEM), pl.BlockSpec(), held, held],
        out_shape=[jax.ShapeDtypeStruct((PAYLOAD, HD), BF), jax.ShapeDtypeStruct((8, HD), F32)],
        scratch_shapes=[pltpu.VMEM((PRE, HD), BF), pltpu.VMEM((PRE, HD), BF), pltpu.SemaphoreType.DMA((2, OWN_COPIES))],
        compiler_params=pltpu.CompilerParams(vmem_limit_bytes=59 << 20),
        cost_estimate=pl.CostEstimate(
            flops=4 * QROWS * PRE * HD, bytes_accessed=2 * 2 * PRE * HD, transcendentals=QROWS * PRE
        ),
        name="own_prefix",
    )(group, q, keys, values)


def prefix_part(group, q, which, keys, values, after):
    vmem = pl.BlockSpec(memory_space=pltpu.VMEM)
    return pl.pallas_call(
        functools.partial(prefix_kernel, which),
        in_specs=[pl.BlockSpec(memory_space=pltpu.SMEM), pl.BlockSpec(), vmem, vmem]
        + [pl.BlockSpec(memory_space=pl.ANY)] * len(after),
        out_shape=jax.ShapeDtypeStruct((PAYLOAD, HD), BF),
        compiler_params=pltpu.CompilerParams(vmem_limit_bytes=VMEM),
        cost_estimate=pl.CostEstimate(
            flops=4 * QROWS * PRE * HD, bytes_accessed=2 * 2 * PRE * HD, transcendentals=QROWS * PRE
        ),
        name="prefix_part",
    )(group, q, keys, values, *after)


def pair_kernel(mine_ref, across_ref, _, out_ref):
    out_ref[0] = mine_ref[...]
    out_ref[1] = across_ref[...]


def pair_up(mine, across, after):
    return pl.pallas_call(
        pair_kernel,
        out_shape=jax.ShapeDtypeStruct((2, *mine.shape), mine.dtype),
        compiler_params=pltpu.CompilerParams(vmem_limit_bytes=VMEM),
        cost_estimate=pl.CostEstimate(flops=0, bytes_accessed=4 * mine.size * 2, transcendentals=0),
        name="pair_up",
    )(mine, across, after)


SUF_LEAVES = 16


def suffix_kernel(q_ref, k_ref, v_ref, nk_ref, nv_ref, len_ref, o_ref, lse_ref):
    scale = 1.0 / (HD**0.5)
    n = SUF_LEAVES * GROUP
    q = heads_as_rows(q_ref[...])
    s = nt_dot(q, k_ref[...]) * scale
    lengths = jnp.concatenate([len_ref[...][:, :1]] * GROUP, axis=0)
    row = lax.broadcasted_iota(jnp.int32, (n, 1), 0) % SUF_LEAVES
    slot = lax.broadcasted_iota(jnp.int32, s.shape, 1) - row * SUF
    s = jnp.where((slot >= 0) & (slot < lengths), s, -1e30)
    fresh_key = jnp.concatenate([nk_ref[...].astype(F32)] * GROUP, axis=0)
    fresh = jnp.sum(q.astype(F32) * fresh_key, axis=1, keepdims=True) * scale
    top = jnp.maximum(jnp.max(s, axis=1, keepdims=True), fresh)
    w = jnp.exp(s - top)
    wn = jnp.exp(fresh - top)
    total = jnp.sum(w, axis=1, keepdims=True) + wn
    o = jnp.dot(w.astype(BF), v_ref[...], preferred_element_type=F32)
    fresh_value = jnp.concatenate([nv_ref[...].astype(F32)] * GROUP, axis=0)
    o = (o + wn.astype(BF).astype(F32) * fresh_value) / total
    lse = jnp.broadcast_to(top + jnp.log(total), o.shape)
    for h in range(GROUP):
        o_ref[h] = o[h * SUF_LEAVES : (h + 1) * SUF_LEAVES]
        lse_ref[h] = lse[h * SUF_LEAVES : (h + 1) * SUF_LEAVES]


def suffix_part(q, keys, values, new_key, new_value, lengths):
    shape = jax.ShapeDtypeStruct((GROUP, ROWS, HD), F32)
    leaf = lambda w: pl.BlockSpec((SUF_LEAVES, w), lambda i: (i, 0))
    cached = pl.BlockSpec((SUF_LEAVES * SUF, HD), lambda i: (i, 0))
    return pl.pallas_call(
        suffix_kernel,
        grid=(ROWS // SUF_LEAVES,),
        in_specs=[leaf(GROUP * HD), cached, cached, leaf(HD), leaf(HD), leaf(HD)],
        out_specs=[pl.BlockSpec((GROUP, SUF_LEAVES, HD), lambda i: (0, i, 0))] * 2,
        out_shape=[shape, shape],
        compiler_params=pltpu.CompilerParams(vmem_limit_bytes=VMEM),
        cost_estimate=pl.CostEstimate(flops=4 * QROWS * 2048 * HD, bytes_accessed=4 << 20, transcendentals=QROWS * 2048),
        name="suffix_part",
    )(
        q,
        keys.reshape(ROWS * SUF, HD),
        values.reshape(ROWS * SUF, HD),
        new_key,
        new_value,
        jnp.broadcast_to(lengths[:, None], (ROWS, HD)),
    )


def merge_kernel(*refs):
    parts, (so_ref, sl_ref, out_ref, held) = refs[:KV], refs[KV:]

    def rows_of(at, n):
        return [p[at : at + n, :].astype(F32) for p in parts]

    for t in range(QROWS // 128):
        rows = [m[0:1] + m[1:2] + m[2:3] for m in rows_of(QROWS + t * META, META)]
        lse = jnp.concatenate(rows, axis=0).T
        suf_lse = sl_ref[t * 128 : (t + 1) * 128, :1]
        top = jnp.maximum(jnp.max(lse, axis=1, keepdims=True), suf_lse)
        w = jnp.exp(lse - top)
        ws = jnp.exp(suf_lse - top)
        total = jnp.sum(w, axis=1, keepdims=True) + ws
        o = so_ref[t * 128 : (t + 1) * 128, :] * ws
        for i, p in enumerate(rows_of(t * 128, 128)):
            o = o + p * w[:, i : i + 1]
        held[t * 128 : (t + 1) * 128, :] = (o / total).astype(BF)
    for n in range(8):
        for h in range(GROUP):
            out_ref[n, :, h * HD : (h + 1) * HD] = held[h * ROWS : (h + 1) * ROWS, :]


def merge_parts(parts, suffix_out, suffix_lse):
    return pl.pallas_call(
        merge_kernel,
        out_shape=jax.ShapeDtypeStruct((8, ROWS, GROUP * HD), BF),
        scratch_shapes=[pltpu.VMEM((QROWS, HD), BF)],
        compiler_params=pltpu.CompilerParams(vmem_limit_bytes=VMEM),
        cost_estimate=pl.CostEstimate(flops=QROWS * HD * 20, bytes_accessed=2 << 20, transcendentals=QROWS * 10),
        name="merge_parts",
    )(*parts, suffix_out.reshape(QROWS, HD), suffix_lse.reshape(QROWS, HD))


def project_kernel(z_ref, a_ref, own_w_ref, other_w_ref, g0_ref, g1_ref, gain_ref, mine_ref, *send_refs):
    gain_ref[:, :HALF] = g0_ref[...].astype(F32)
    gain_ref[:, HALF:] = g1_ref[...].astype(F32)
    z = z_ref[0]
    pieces = [a_ref[pl.ds(pl.multiple_of((z + s) % 4 * 96, 16), 96), :] for s in range(4)]
    a = jnp.concatenate(pieces, axis=0)
    for half, w_ref in enumerate((own_w_ref, other_w_ref)):
        y = jnp.dot(a, w_ref[...], preferred_element_type=F32)
        at = slice(half * HALF, (half + 1) * HALF)
        mine_ref[:, at] = y[:96]
        for s, ref in enumerate(send_refs):
            ref[:, at] = y[(s + 1) * 96 : (s + 2) * 96].astype(BF)


def project(z, attended, own_w, other_w, own_gain, other_gain):
    vmem = pl.BlockSpec(memory_space=pltpu.VMEM)
    return pl.pallas_call(
        project_kernel,
        in_specs=[pl.BlockSpec(memory_space=pltpu.SMEM)] + [vmem] * 5,
        out_specs=[vmem] * 5,
        out_shape=[jax.ShapeDtypeStruct((1, 2 * HALF), F32), jax.ShapeDtypeStruct((96, 2 * HALF), F32)] + [jax.ShapeDtypeStruct((96, 2 * HALF), BF)] * 3,
        compiler_params=pltpu.CompilerParams(vmem_limit_bytes=VMEM),
        cost_estimate=pl.CostEstimate(flops=2 * 384 * 1024 * 1024, bytes_accessed=4 << 20, transcendentals=0),
        name="project",
    )(z, attended, own_w, other_w, own_gain, other_gain)


def fill_kernel(place_ref, *refs):
    pieces, (gain_ref, scaled_ref, squares_ref, theirs_ref) = refs[:4], refs[4:]
    for j, piece in enumerate(pieces):
        for e in range(2):
            sent = pl.multiple_of(place_ref[j * 2 + e] * ROWS, 16)
            block = pl.multiple_of(place_ref[8 + j * 2 + e] * ROWS, 16)
            rows = piece[e * ROWS : (e + 1) * ROWS, :]
            wide = rows.astype(F32)
            scaled_ref[pl.ds(sent, ROWS), :] = (wide * gain_ref[...]).astype(BF)
            theirs_ref[pl.ds(block, ROWS), :] = rows[:, HALF:]
            squares = jnp.sum(wide * wide, axis=1, keepdims=True)
            squares_ref[pl.ds(sent, ROWS), :] = jnp.broadcast_to(squares, (ROWS, HD))


def fill(place, pieces, gain):
    vmem = pl.BlockSpec(memory_space=pltpu.VMEM)
    return pl.pallas_call(
        fill_kernel,
        in_specs=[pl.BlockSpec(memory_space=pltpu.SMEM)] + [vmem] * 5,
        out_shape=[
            jax.ShapeDtypeStruct((384, 2 * HALF), BF),
            jax.ShapeDtypeStruct((384, HD), F32),
            jax.ShapeDtypeStruct((384, HALF), BF),
        ],
        compiler_params=pltpu.CompilerParams(vmem_limit_bytes=VMEM),
        cost_estimate=pl.CostEstimate(flops=384 * 4096, bytes_accessed=2 << 20, transcendentals=0),
        name="scale_rows",
    )(place, *pieces, gain)


def assemble_kernel(place_ref, *refs):
    pieces, (theirs_ref, out_ref, token_ref) = refs[:4], refs[4:]
    token_ref[...] = jnp.zeros_like(token_ref)
    core = place_ref[16]
    for j, piece in enumerate(pieces):
        for e in range(2):
            block = place_ref[8 + j * 2 + e]
            ours = pl.multiple_of((block * 2 + core) * ROWS, 16)
            other = pl.multiple_of((block * 2 + 1 - core) * ROWS, 16)
            out_ref[pl.ds(ours, ROWS), :] = piece[e * ROWS : (e + 1) * ROWS, :HALF]
            out_ref[pl.ds(other, ROWS), :] = theirs_ref[pl.ds(pl.multiple_of(block * ROWS, 16), ROWS), :]


def assemble(place, pieces, theirs):
    return pl.pallas_call(
        assemble_kernel,
        in_specs=[pl.BlockSpec(memory_space=pltpu.SMEM)] + [pl.BlockSpec()] * 5,
        out_shape=[jax.ShapeDtypeStruct((768, HALF), BF), jax.ShapeDtypeStruct((8, HD), F32)],
        compiler_params=pltpu.CompilerParams(vmem_limit_bytes=VMEM),
        cost_estimate=pl.CostEstimate(flops=1000, bytes_accessed=1000, transcendentals=0),
        name="assemble_stream",
    )(place, *pieces, theirs)


def hold_kernel(_, *refs):
    sources, places, sems = refs[:4], refs[4:8], refs[8]
    copies = [pltpu.make_async_copy(a, b, sems.at[i]) for i, (a, b) in enumerate(zip(sources, places))]
    for copy in copies:
        copy.start()
    for copy in copies:
        copy.wait()


def hold(after, *arrays):
    return pl.pallas_call(
        hold_kernel,
        in_specs=[pl.BlockSpec()] + [pl.BlockSpec(memory_space=pl.ANY)] * 4,
        out_specs=[pl.BlockSpec(memory_space=pltpu.VMEM)] * 4,
        out_shape=[jax.ShapeDtypeStruct(a.shape, a.dtype) for a in arrays],
        scratch_shapes=[pltpu.SemaphoreType.DMA((4,))],
        compiler_params=pltpu.CompilerParams(vmem_limit_bytes=24 << 20),
        cost_estimate=pl.CostEstimate(flops=0, bytes_accessed=sum(a.size * 4 for a in arrays), transcendentals=0),
        name="hold_weights",
    )(after, *arrays)


def weight_tiles(first, columns, weights):
    ends = range(columns % TILE or TILE, columns + 1, TILE)
    for end in ends:
        at = slice(max(end - TILE, 0), end)
        yield at, [w[:, first + at.start : first + at.stop] for w in weights]


def hidden_sums(s, own_gate, other_gate, own_up, other_up):
    out = []
    for own, other in ((own_gate, other_gate), (own_up, other_up)):
        y = jnp.dot(s[:, :HALF], own, preferred_element_type=F32)
        out.append(y + jnp.dot(s[:, HALF:], other, preferred_element_type=F32))
    return out


def x_first_kernel(first, columns, s_ref, g0, g1, u0, u1, *refs):
    keep_ref, send_ref, token_ref = refs[-3:]
    token_ref[...] = jnp.zeros_like(token_ref)
    for to, blocks in weight_tiles(first, columns, (g0, g1, u0, u1)):
        for n, y in enumerate(hidden_sums(s_ref[...], *blocks)):
            for k in range(4):
                keep_ref[k, n, :, to] = y[k * ROWS : (k + 1) * ROWS].astype(BF)
                send_ref[k, n, :, to] = y[(4 + k) * ROWS : (5 + k) * ROWS].astype(BF)


def y_first_kernel(first, columns, s_ref, g0, g1, u0, u1, squares_ref, *refs):
    here_ref, up_add, up_pass, down_add, down_pass, far_gate, far_up = refs
    up, down, far = (up_add, up_pass), (down_pass, down_add), (far_gate, far_up)

    def put(n, to, y):
        for x in range(2):
            at = slice(x * ROWS, (x + 1) * ROWS)
            part = [y[(x * 4 + k) * ROWS : (x * 4 + k + 1) * ROWS] for k in range(4)]
            here_ref[at, to.start + n * (columns + HD) : to.stop + n * (columns + HD)] = part[0].astype(BF)
            for ref, value in ((up[n], part[1]), (far[n], part[2]), (down[n], part[3])):
                ref[at, to] = value.astype(BF)

    put(0, slice(columns, columns + HD), squares_ref[...])
    for to, blocks in weight_tiles(first, columns, (g0, g1, u0, u1)):
        for n, y in enumerate(hidden_sums(s_ref[...], *blocks)):
            put(n, to, y)


def hidden_call(kernel, first, columns, scaled, weights, shapes, flops, name, more):
    return pl.pallas_call(
        functools.partial(kernel, first, columns),
        in_specs=[pl.BlockSpec()] + [pl.BlockSpec(memory_space=pltpu.VMEM)] * 4 + [pl.BlockSpec()] * len(more),
        out_shape=shapes,
        compiler_params=pltpu.CompilerParams(vmem_limit_bytes=12 << 20),
        cost_estimate=pl.CostEstimate(flops=flops, bytes_accessed=flops // 1000, transcendentals=0),
        name=name,
    )(scaled, *weights, *more)


def x_first(first, columns, scaled, weights, *after):
    shapes = [jax.ShapeDtypeStruct((4, 2, ROWS, columns), BF)] * 2 + [jax.ShapeDtypeStruct((8, HD), F32)]
    return hidden_call(
        x_first_kernel, first, columns, scaled, weights, shapes, 10**8, "hidden_x_first", after
    )


def y_first(first, columns, scaled, weights, squares):
    gate, rows = columns + HD, 2 * ROWS
    parts = [gate + columns, gate, columns, columns, gate, gate, columns]
    shapes = [jax.ShapeDtypeStruct((rows, n), BF) for n in parts]
    return hidden_call(
        y_first_kernel, first, columns, scaled, weights, shapes, 10**9, "hidden_y_first", (squares,)
    )


def pass_on_kernel(up_add, down_add, below, above, _, to_above, to_below):
    to_above[...] = (up_add[...].astype(F32) + below[...].astype(F32)).astype(BF)
    to_below[...] = (down_add[...].astype(F32) + above[...].astype(F32)).astype(BF)


def pass_on(*sums):
    shapes = [jax.ShapeDtypeStruct(v.shape, BF) for v in sums[:2]]
    return pl.pallas_call(
        pass_on_kernel,
        out_shape=shapes,
        compiler_params=pltpu.CompilerParams(vmem_limit_bytes=VMEM),
        cost_estimate=pl.CostEstimate(flops=1000, bytes_accessed=1000, transcendentals=0),
        name="pass_on_sums",
    )(*sums)


def finish_kernel(here_ref, below_gate, below_up, above_gate, above_up, _, keep_ref, send_ref):
    gate = below_gate.shape[1]
    for at, below, above in ((slice(0, gate), below_gate, above_gate), (slice(gate, None), below_up, above_up)):
        sums = here_ref[:, at].astype(F32) + below[...].astype(F32) + above[...].astype(F32)
        keep_ref[:, at] = sums[:ROWS]
        send_ref[:, at] = sums[ROWS:].astype(BF)


def finish_y(here, received, after):
    shape = lambda t: jax.ShapeDtypeStruct((ROWS, here.shape[1]), t)
    return pl.pallas_call(
        finish_kernel,
        out_shape=[shape(F32), shape(BF)],
        compiler_params=pltpu.CompilerParams(vmem_limit_bytes=VMEM),
        cost_estimate=pl.CostEstimate(flops=1000, bytes_accessed=1000, transcendentals=0),
        name="finish_y",
    )(here, *received, after)


def add_kernel(keep_ref, got_ref, _, mine_ref, *send_refs):
    for k, ref in enumerate((mine_ref, *send_refs)):
        ref[...] = (keep_ref[k].astype(F32) + got_ref[k].astype(F32)).astype(ref.dtype)


def add_got(keep, got, after):
    held = pl.BlockSpec(memory_space=pl.ANY)
    return pl.pallas_call(
        add_kernel,
        in_specs=[pl.BlockSpec(), pl.BlockSpec(), held],
        out_shape=[jax.ShapeDtypeStruct(keep.shape[1:], t) for t in (F32, BF, BF, BF)],
        compiler_params=pltpu.CompilerParams(vmem_limit_bytes=VMEM),
        cost_estimate=pl.CostEstimate(flops=1000, bytes_accessed=1000, transcendentals=0),
        name="add_across_x",
    )(keep, got, after)


def activate(gate, up, rms):
    return (jax.nn.silu(gate / rms) * (up / rms)).astype(BF)


def finish_b_kernel(keep_ref, got_ref, out_ref, rms_ref):
    columns = out_ref.shape[1]
    sums = keep_ref[...] + got_ref[...].astype(F32)
    rms = jnp.sqrt(sums[:, columns : columns + HD] / D + 1e-05)
    rms_ref[...] = rms
    out_ref[...] = activate(sums[:, :columns], sums[:, columns + HD :], rms[:, :1])


def finish_b(keep, got):
    return pl.pallas_call(
        finish_b_kernel,
        out_shape=[jax.ShapeDtypeStruct((ROWS, B_COLS), BF), jax.ShapeDtypeStruct((ROWS, HD), F32)],
        compiler_params=pltpu.CompilerParams(vmem_limit_bytes=VMEM),
        cost_estimate=pl.CostEstimate(flops=10**6, bytes_accessed=1 << 20, transcendentals=10**5),
        name="finish_b",
    )(keep, got)


def finish_a_kernel(mine_ref, *refs):
    got, (b_ref, rms_ref, out_ref) = refs[:3], refs[3:]
    gate, up = (mine_ref[n] + sum(g[n].astype(F32) for g in got) for n in range(2))
    out_ref[:, :A_COLS] = activate(gate, up, rms_ref[:, :1])
    out_ref[:, A_COLS:] = b_ref[...]


def finish_a(mine, got, b_part, rms):
    return pl.pallas_call(
        finish_a_kernel,
        out_shape=jax.ShapeDtypeStruct((ROWS, HIDDEN), BF),
        compiler_params=pltpu.CompilerParams(vmem_limit_bytes=VMEM),
        cost_estimate=pl.CostEstimate(flops=10**6, bytes_accessed=1 << 20, transcendentals=10**5),
        name="finish_a",
    )(mine, *got, b_part, rms)


def y_sums(up_add, up_pass, down_add, down_pass, far_gate, far_up, token):
    from_below = over_batch(far_gate, 0, 1)
    from_above = over_batch(far_up, 0, -1)
    gate_above, up_below = pass_on(up_add, down_add, from_below, from_above, token)
    above = over_batch(gate_above, 0, 1), over_batch(up_pass, 0, 1)
    below = over_batch(down_pass, 0, -1), over_batch(up_below, 0, -1)
    return (*above, *below)


def on_device(
    queries,
    new_key,
    new_value,
    prefix_keys,
    prefix_values,
    suffix_keys,
    suffix_values,
    suffix_lengths,
    out_weight,
    residual,
    norm_gain,
    gate_weight,
    up_weight,
):
    c = lax.axis_index("ctx")
    b = lax.axis_index("batch")
    xh, z = c // 4, c % 4
    xl, y, core = b // 8, b // 2 % 4, b % 2

    other_gate, other_up = over_batch(gate_weight, 0, 0, 1), over_batch(up_weight, 0, 0, 1)
    other_out = over_batch(out_weight, 0, 0, 1)
    own_gain = norm_gain.reshape(1, HALF)
    other_gain = over_batch(own_gain, 0, 0, 1)
    blocks = residual.reshape(4, 2, 2, ROWS, HALF)
    take = lambda k: lax.dynamic_slice(blocks, (z, 0, k, 0, 0), (1, 2, 1, ROWS, HALF)).reshape(96, HALF)
    residual_rows = jnp.concatenate([take(core), over_batch(take(1 - core), 0, 0, 1)], axis=1)

    def group_of(flip, s):
        return ((xh + flip) % 2 * 4 + (z - s) % 4).astype(jnp.int32).reshape(1)

    q_across = over_ctx(queries, 1, 0)
    own, token = own_prefix(group_of(0, 0), queries, prefix_keys, prefix_values)
    q2 = pair_up(queries, q_across, token)
    arrived = {0: None} | {s: over_ctx(q2, 0, s) for s in (1, 3, 2)}
    across = prefix_part(group_of(1, 0), q_across, None, prefix_keys, prefix_values, ())
    suffix_out, suffix_lse = suffix_part(queries, suffix_keys, suffix_values, new_key, new_value, suffix_lengths)
    parts, last = [own, over_ctx(across, 1, 0)], across
    for s in (1, 3, 2):
        for flip in (1, 0):
            after = (last,) if len(parts) < 5 else (last, parts[len(parts) - 4])
            group = group_of(flip, s)
            if len(parts) == 2:
                group, other_gate, other_up = lax.optimization_barrier((group, other_gate, other_up))
            last = prefix_part(group, arrived[s], flip, prefix_keys, prefix_values, after)
            parts.append(over_ctx(last, flip, -s))
    attended = merge_parts(parts, suffix_out, suffix_lse)
    everyone = lax.all_to_all(
        attended,
        "batch",
        0,
        0,
        axis_index_groups=SAME_CORE,
        tiled=True,
    ).reshape(384, 1024)
    gain, mine, *send = project(
        z.astype(jnp.int32).reshape(1), everyone, out_weight, other_out, own_gain, other_gain
    )
    for s in (1, 3, 2):
        mine = mine + over_ctx(send[s - 1], 0, s).astype(F32)
    mine = mine.astype(BF)
    across = over_ctx(mine, 1, 0)
    mixed = mine.astype(F32) + across.astype(F32)
    chunk = (residual_rows.astype(F32) + mixed).astype(BF)
    pieces = [chunk] + [over_ctx(chunk, 0, s) for s in (1, 3, 2)]
    piece_z = [z, (z - 1) % 4, (z - 3) % 4, (z - 2) % 4]

    blocks = [2 * pz + e for pz in piece_z for e in range(2)]
    place = [(block // 4 - xl) % 2 * 4 + (block % 4 - y) % 4 for block in blocks] + blocks + [core]
    place = jnp.stack(place).astype(jnp.int32)
    scaled, squares, their_columns = fill(place, pieces, gain)
    weights = hold(chunk, gate_weight, other_gate, up_weight, other_up)
    b_first = y_first(A_COLS, B_COLS, scaled, weights, squares)
    a_first = x_first(0, A_COLS, scaled, weights, b_first[-1])
    received = y_sums(*b_first[1:], a_first[2])
    stream, token = assemble(place, pieces, over_batch(their_columns, 0, 0, 1))
    b_keep, b_send = finish_y(b_first[0], received, token)
    b_part, rms = finish_b(b_keep, over_batch(b_send, 1, 0))
    mine, *sends = add_got(a_first[0], over_batch(a_first[1], 1, 0), token)
    activation = finish_a(mine, [over_batch(sends[s - 1], 0, s) for s in (2, 1, 3)], b_part, rms)
    return (stream, activation)


def solution(mesh):
    in_specs = (
        P("batch", "ctx"),
        P("batch", "ctx"),
        P("batch", "ctx"),
        P("ctx", None),
        P("ctx", None),
        P("batch", None, "ctx"),
        P("batch", None, "ctx"),
        P("batch"),
        P("ctx", "batch"),
        P(None, "batch"),
        P("batch"),
        P("batch", "ctx"),
        P("batch", "ctx"),
    )
    out_specs = (P(None, "batch"), P("batch", "ctx"))
    return jax.shard_map(
        on_device, mesh=mesh, in_specs=in_specs, out_specs=out_specs, check_vma=False
    )
```
